256 devices in a mesh: ctx: 128 (over y_lo, x, z, core), dp: 2 (over y_hi).
Axes of the slice: x: 4, y: 4 (y_hi: 2, y_lo: 2; y = y_hi * 2 + y_lo), z: 8, core: 2. Of those that a mesh axis runs over, the one named last changes fastest.
Arguments:
- queries: bfloat16 [32768, 1024], P(('dp', 'ctx')), parts along dimension 0, may hold values from -6 to 6
- keys: bfloat16 [32768, 1024], P(('dp', 'ctx')), parts along dimension 0, may hold values from -6 to 6
- values: bfloat16 [32768, 1024], P(('dp', 'ctx')), parts along dimension 0, may hold values from -6 to 6
- cotangent: bfloat16 [32768, 1024], P(('dp', 'ctx')), parts along dimension 0, may hold values from -6 to 6
- doc_lengths: int32 [128], P('dp'), parts along dimension 0, may hold values from 1 to 512, 16384 in all
Outputs:
- attended: bfloat16 [32768, 1024], P(('dp', 'ctx')), parts along dimension 0
- query_grad: bfloat16 [32768, 1024], P(('dp', 'ctx')), parts along dimension 0
- key_grad: bfloat16 [32768, 1024], P(('dp', 'ctx')), parts along dimension 0
- value_grad: bfloat16 [32768, 1024], P(('dp', 'ctx')), parts along dimension 0
The draws below stay inside these ranges and needn't reach their ends.
There are 2 independent parts, one for each index of `dp`. The reference program is written for one: setup_inputs(seed, part) draws one part's arguments, and reference() takes and returns one part's arrays. A program takes and returns all parts, laid end to end along the dimension named above; each array names one. Nothing has to cross between parts.
Inputs may be any that keep to these rules, and one draw needn't show every extreme that they name: `doc_lengths`: the 64 lengths sum to 16384; the longest is exactly 512.
All inputs are finite; a program needn't handle non-finite values.
Results may differ from the reference program's by a relative error of at most 0.027.
Values may be sent and summed in bfloat16 or wider, within the bound.
A program may use at most 64 MiB of HBM per device.

```python
import math
import jax
import jax.numpy as jnp
import numpy as np
from jax import lax

H = 16
DH = 64
D = 1024
TOK_DEV = 128
REACH = 4
TOKENS = 16384
DOCS = 64
N_CTX = 128


def draw_queries(key, part):
    key = jax.random.fold_in(key, 1)
    base = jax.random.normal(key, (TOKENS, D), jnp.float32)
    return jnp.clip(base, -6.0, 6.0).astype(jnp.bfloat16)


def draw_keys(key, part):
    key = jax.random.fold_in(key, 2)
    base = jax.random.normal(key, (TOKENS, D), jnp.float32)
    return jnp.clip(base, -6.0, 6.0).astype(jnp.bfloat16)


def level_of(stream_key, extent, cuts, low, top_value):
    factor_of = 1.0
    for dim, blocks in cuts:
        steps = jax.random.uniform(jax.random.fold_in(jax.random.fold_in(stream_key, 6), dim), (blocks,), jnp.float32, low / len(cuts), top_value / len(cuts))
        factor_of = factor_of * jnp.repeat(jnp.exp(steps), extent[dim] // blocks).reshape((-1,) + (1,) * (len(extent) - 1 - dim))
    return factor_of


def length_profile(amount, total, reach, skew):
    portions = [(1 << 20) // math.isqrt(rank ** skew) + 1 for rank in range(2, amount + 1)]
    rest, given = total - reach - (amount - 1), [1] * (amount - 1)
    while rest > 0:
        movable = [i for i in range(amount - 1) if given[i] < reach]
        mass, remaining = sum([portions[i] for i in movable]), rest
        for i in movable:
            more = min(reach - given[i], max(1, remaining * portions[i] // mass), rest)
            given[i] = given[i] + more
            rest = rest - more
    return np.array([reach] + given)


def uneven(stream_key, amount, total, reach, lean):
    if amount == 2:
        one = jax.random.randint(stream_key, (), max(1, total - reach), min(reach, total - 1) + 1)
        return jnp.stack([one, total - one])
    sizes = jnp.asarray(length_profile(amount, total, reach, lean), jnp.int32)
    twos = (amount - 1) // 2
    source_of, taker = sizes[1:1 + 2 * twos:2], sizes[2:2 + 2 * twos:2]
    room = jnp.minimum(source_of - 1, reach - taker)
    shifted = jax.random.randint(jax.random.fold_in(stream_key, 1), (twos,), 0, 1 << 20) % (room + 1)
    sizes = sizes.at[1:1 + 2 * twos:2].set(source_of - shifted).at[2:2 + 2 * twos:2].set(taker + shifted)
    return sizes[jax.random.permutation(jax.random.fold_in(stream_key, 2), amount)]


def noise(stream_key, extent, scale, most, cuts=(), kind=jnp.bfloat16):
    gain = level_of(stream_key, extent, cuts, -0.22, 0.18) if cuts else 1.0
    result = jax.random.normal(stream_key, extent, jnp.float32) * scale * gain
    return jnp.minimum(jnp.maximum(result, -most), most).astype(kind)


def setup_inputs(seed: int = 0, part: int = 0) -> dict:
    key_list = jax.random.split(jax.random.key(seed), 6)
    own_keys = jax.random.split(jax.random.fold_in(key_list[5], part), 6)
    queries = draw_queries(jax.random.fold_in(jax.random.fold_in(key_list[5], part), 71), part)
    keys = draw_keys(jax.random.fold_in(jax.random.fold_in(key_list[5], part), 71), part)
    values = noise(own_keys[2], (TOKENS, D), 1.0, 6.0, ((0, 128),))
    cotangent = noise(own_keys[3], (TOKENS, D), 1.0, 6.0, ((0, 128),))
    doc_lengths = uneven(own_keys[4], DOCS, TOKENS, REACH * TOK_DEV, 2).astype(jnp.int32)
    return dict(queries=queries, keys=keys, values=values, cotangent=cotangent, doc_lengths=doc_lengths)


def segment_ids(doc_ends, start, count, total_tokens):
    position = start + jnp.arange(count, dtype=jnp.int32)
    found = jnp.sum((doc_ends[None, :] <= position[:, None]).astype(jnp.int32), axis=1)
    inside = (position >= 0) & (position < total_tokens)
    return jnp.where(inside, found, -1).astype(jnp.int32)


def shares_document(query_ids, key_ids):
    key_high = jnp.max(key_ids)
    key_low = jnp.min(jnp.where(key_ids >= 0, key_ids, 1 << 30))
    return (key_high >= jnp.min(query_ids)) & (key_low <= jnp.max(query_ids))


def reference(queries, keys, values, cotangent, doc_lengths):
    row_count = TOK_DEV
    block_count = N_CTX
    total_tokens = TOKENS
    score_scale = float(DH) ** -0.5
    doc_ends = jnp.cumsum(doc_lengths).astype(jnp.int32)
    margin = REACH * row_count

    def padded_blocks(source):
        padded = jnp.pad(source.astype(jnp.float32), ((margin, margin), (0, 0)))
        return padded.reshape(block_count + 2 * REACH, row_count, H, DH)

    key_blocks = padded_blocks(keys)
    value_blocks = padded_blocks(values)
    query_all = queries.astype(jnp.float32).reshape(block_count, row_count, H, DH)
    cotangent_all = cotangent.astype(jnp.float32).reshape(block_count, row_count, H, DH)
    offsets = [0] + list(range(1, REACH + 1)) + [-d for d in range(1, REACH + 1)]

    def step(accumulated, block):
        query_heads = lax.dynamic_index_in_dim(query_all, block, 0, keepdims=False)
        cotangent_heads = lax.dynamic_index_in_dim(cotangent_all, block, 0, keepdims=False)
        query_ids = segment_ids(doc_ends, block * row_count, row_count, total_tokens)
        tiles = []
        for offset in offsets:
            key_heads = lax.dynamic_index_in_dim(key_blocks, block + offset + REACH, 0, keepdims=False)
            value_heads = lax.dynamic_index_in_dim(value_blocks, block + offset + REACH, 0, keepdims=False)
            key_ids = segment_ids(doc_ends, (block + offset) * row_count, row_count, total_tokens)
            tiles.append((key_heads, value_heads, key_ids, shares_document(query_ids, key_ids)))

        def scores_of(key_heads, key_ids):
            scores = jnp.einsum("qhd,khd->hqk", query_heads, key_heads) * score_scale
            same = query_ids[:, None] == key_ids[None, :]
            return jnp.where(same[None], scores, -jnp.inf)

        row_max = jnp.full((H, row_count), -jnp.inf, jnp.float32)
        row_sum = jnp.zeros((H, row_count), jnp.float32)
        for key_heads, value_heads, key_ids, shared in tiles:
            def update(state, key_heads=key_heads, key_ids=key_ids):
                scores = scores_of(key_heads, key_ids)
                new_max = jnp.maximum(state[0], jnp.max(scores, axis=2))
                new_sum = state[1] * jnp.exp(state[0] - new_max) + jnp.sum(jnp.exp(scores - new_max[:, :, None]), axis=2)
                return (new_max, new_sum)
            row_max, row_sum = lax.cond(shared, update, lambda state: state, (row_max, row_sum))
        lse = row_max + jnp.log(row_sum)

        output = jnp.zeros((row_count, H, DH), jnp.float32)
        for key_heads, value_heads, key_ids, shared in tiles:
            def add_out(state, key_heads=key_heads, value_heads=value_heads, key_ids=key_ids):
                probs_low = jnp.exp(scores_of(key_heads, key_ids) - lse[:, :, None]).astype(jnp.bfloat16)
                return state + jnp.einsum("hqk,khd->qhd", probs_low.astype(jnp.float32), value_heads)
            output = lax.cond(shared, add_out, lambda state: state, output)
        attended_heads = output.astype(jnp.bfloat16)
        row_delta = jnp.sum(cotangent_heads * attended_heads.astype(jnp.float32), axis=2).T

        query_total = jnp.zeros((row_count, H, DH), jnp.float32)
        for index_tile, (key_heads, value_heads, key_ids, shared) in enumerate(tiles):
            offset = offsets[index_tile]

            def backward(state, key_heads=key_heads, value_heads=value_heads, key_ids=key_ids):
                probs = jnp.exp(scores_of(key_heads, key_ids) - lse[:, :, None])
                probs_low = probs.astype(jnp.bfloat16).astype(jnp.float32)
                prob_grads = jnp.einsum("qhd,khd->hqk", cotangent_heads, value_heads)
                score_grads = (probs * (prob_grads - row_delta[:, :, None])).astype(jnp.bfloat16).astype(jnp.float32)
                query_part = jnp.einsum("hqk,khd->qhd", score_grads, key_heads)
                key_part = jnp.einsum("hqk,qhd->khd", score_grads, query_heads) * score_scale
                value_part = jnp.einsum("hqk,qhd->khd", probs_low, cotangent_heads)
                return state[0] + query_part, jnp.stack([key_part, value_part])

            def skipped(state):
                return state[0], jnp.zeros((2, row_count, H, DH), jnp.float32)

            query_total, pieces = lax.cond(shared, backward, skipped, (query_total,))
            if offset != 0:
                pieces = lax.optimization_barrier(pieces.astype(jnp.bfloat16)).astype(jnp.float32)
            where = (block + offset + REACH).astype(jnp.int32)
            current = lax.dynamic_index_in_dim(accumulated, where, 0, keepdims=False)
            accumulated = lax.dynamic_update_index_in_dim(accumulated, current + pieces, where, 0)
        query_grad = (query_total * score_scale).astype(jnp.bfloat16)
        return accumulated, (attended_heads, query_grad)

    start = jnp.zeros((block_count + 2 * REACH, 2, row_count, H, DH), jnp.float32)
    accumulated, (attended, query_grad) = lax.scan(step, start, jnp.arange(block_count, dtype=jnp.int32))
    owned = accumulated[REACH:REACH + block_count]
    key_grad = owned[:, 0].reshape(total_tokens, H * DH).astype(jnp.bfloat16)
    value_grad = owned[:, 1].reshape(total_tokens, H * DH).astype(jnp.bfloat16)
    return (attended.reshape(total_tokens, H * DH), query_grad.reshape(total_tokens, H * DH), key_grad, value_grad)
```

```python
import functools

import jax
import jax.numpy as jnp
from jax import lax
from jax.experimental import pallas as pl
from jax.experimental.pallas import tpu as pltpu
from jax.sharding import PartitionSpec as P

H = 16
DH = 64
ROWS = 128
CHIP = 2 * ROWS
HEADS = H // 2
LAG = 2
SLOTS = HEADS + LAG
CHUNK = 256
LOG2E = 1.4426950408889634
F32 = jnp.float32
BF16 = jnp.bfloat16


def low_lanes(shape):
    return lax.broadcasted_iota(jnp.int32, shape, 1) < DH


def join(left, right, half):
    lanes = slice(0, DH) if half == 0 else slice(DH, 2 * DH)
    return jnp.concatenate([left[:, lanes], right[:, lanes]], axis=1)


def token_info(ends, base, axis, total):
    shape = (CHIP, 1) if axis == 0 else (1, CHIP)
    place = lax.broadcasted_iota(jnp.int32, shape, axis).astype(F32) + base
    before = ends <= place
    start = jnp.max(jnp.where(before, ends, 0.0), axis=1 - axis, keepdims=True)
    end = jnp.min(jnp.where(before, 4.0 * total, ends), axis=1 - axis, keepdims=True)
    first = jnp.floor(start * (1.0 / CHIP))
    last = jnp.floor((end - 1.0) * (1.0 / CHIP))
    owner = jnp.minimum(first + 1.0, last)
    inside = (place >= 0.0) & (place < total)
    return start, jnp.where(inside, owner, -9.0)


def kernel(
    n,
    len_ref,
    q_ref,
    k_ref,
    v_ref,
    g_ref,
    o_ref,
    dq_ref,
    dk_ref,
    dv_ref,
    own,
    stage,
    res_own,
    res_nb,
    send_r,
    send_l,
    recv_l,
    recv_r,
    fin,
    fin_out,
    fin_in,
    id_row,
    id_col,
    home,
    guest,
    sib_send,
    sib_recv,
    r_send,
    r_recv,
    l_send,
    l_recv,
    fin_send,
    fin_recv,
):
    me = lax.axis_index("ctx")
    core = lax.rem(me, 2)
    chip = lax.div(me, 2)
    sibling = me + 1 - 2 * core
    right = lax.rem(me + 2, n)
    left = lax.rem(me + n - 2, n)
    mine = pl.ds(pl.multiple_of(core * ROWS, ROWS), ROWS)
    theirs = pl.ds(pl.multiple_of((1 - core) * ROWS, ROWS), ROWS)

    barrier = pltpu.get_barrier_semaphore()
    for other in (sibling, right, left):
        pl.semaphore_signal(barrier, inc=1, device_id={"ctx": other}, device_id_type=pl.DeviceIdType.MESH)
    pl.semaphore_wait(barrier, 3)

    def remote(src, dst, send_sem, recv_sem, target):
        return pltpu.make_async_remote_copy(
            src_ref=src,
            dst_ref=dst,
            send_sem=send_sem,
            recv_sem=recv_sem,
            device_id={"ctx": target},
            device_id_type=pl.DeviceIdType.MESH,
        )

    def exchange(h):
        return remote(stage.at[h], own.at[h, :, mine], sib_send.at[h], sib_recv.at[h], sibling)

    def to_right(s, src):
        return remote(src, recv_l.at[s], r_send.at[s], r_recv.at[s], right)

    def to_left(s, src):
        return remote(src, recv_r.at[s], l_send.at[s], l_recv.at[s], left)

    def hand_back(h):
        return remote(fin_out.at[h], fin_in.at[h], fin_send.at[h], fin_recv.at[h], sibling)

    def packed(pair, half):
        lanes = pl.ds(pl.multiple_of(pair * 2 * DH, 2 * DH), 2 * DH)
        return (
            join(q_ref[:, lanes], g_ref[:, lanes], half),
            join(k_ref[:, lanes], v_ref[:, lanes], half),
        )

    def pack_theirs(pair, _):
        for half in range(2):
            h = 2 * pair + half
            a, b = packed((1 - core) * (HEADS // 2) + pair, half)
            stage[h, 0] = a
            stage[h, 1] = b
            exchange(h).start()
        return 0

    def pack_mine(pair, _):
        for half in range(2):
            h = 2 * pair + half
            a, b = packed(core * (HEADS // 2) + pair, half)
            own[h, 0, mine] = a
            own[h, 1, mine] = b
        return 0

    lax.fori_loop(0, HEADS // 2, pack_theirs, 0)
    lax.fori_loop(0, HEADS // 2, pack_mine, 0)

    for s in range(LAG):
        exchange(s).wait_recv()
        to_right(s, own.at[s]).start()
        to_left(s, own.at[s]).start()

    here = chip.astype(F32)
    total = float(n * ROWS)
    docs = len_ref.shape[1]
    across = lax.broadcasted_iota(jnp.int32, (docs, docs), 1)
    down = lax.broadcasted_iota(jnp.int32, (docs, docs), 0)
    lengths = jnp.broadcast_to(len_ref[...].astype(F32), (docs, docs))
    ends_col = jnp.sum(jnp.where(across <= down, lengths, 0.0), axis=1, keepdims=True)
    ends_row = jnp.sum(jnp.where(across == down, ends_col, 0.0), axis=0, keepdims=True)
    for axis, ends in ((1, ends_col), (0, ends_row)):
        start_o, owner_o = token_info(ends, here * CHIP, axis, total)
        start_l, owner_l = token_info(ends, (here - 1.0) * CHIP, axis, total)
        start_r, owner_r = token_info(ends, (here + 1.0) * CHIP, axis, total)
        id_own = jnp.where(owner_o == here, start_o, -1.0)
        id_nb = jnp.where(owner_l == here, start_l, jnp.where(owner_r == here, start_r, -2.0))
        if axis == 1:
            id_row[:, 0:CHIP] = id_own
            id_row[:, CHIP:] = id_nb
        else:
            id_col[0:CHIP] = jnp.broadcast_to(id_own, (CHIP, 128))
            id_col[CHIP:] = jnp.broadcast_to(id_nb, (CHIP, 128))
            home[...] = jnp.broadcast_to(owner_o - here, (CHIP, 128)).astype(BF16)
            came = jnp.where(owner_l == here, -1.0, jnp.where(owner_r == here, 1.0, 0.0))
            guest[...] = jnp.broadcast_to(came, (CHIP, 128)).astype(BF16)

    def attend(t):
        came = guest[...]
        zero = jnp.zeros((CHIP, 2 * DH), BF16)
        both = []
        for i in range(2):
            nb = jnp.where(came < 0, recv_l[t, i], jnp.where(came > 0, recv_r[t, i], zero))
            both.append(jnp.concatenate([own[t, i], nb], axis=0))
        a, b = both
        at = a.T
        bt = b.T
        none = jnp.zeros((DH, 2 * CHIP), BF16)
        qt = jnp.concatenate([at[:DH], none], axis=0)
        gt = jnp.concatenate([none, at[DH:]], axis=0)
        ids = jnp.concatenate([id_col[...]] * (CHUNK // 128), axis=1)
        low = low_lanes((2 * CHIP, 2 * DH))
        dk = jnp.zeros((2 * CHIP, 2 * DH), F32)
        dv = jnp.zeros((2 * CHIP, 2 * DH), F32)
        for c in range(2 * CHIP // CHUNK):
            part = slice(c * CHUNK, (c + 1) * CHUNK)
            scores = jnp.dot(b, qt[:, part], preferred_element_type=F32)
            scores = jnp.where(ids == id_row[:, part], scores, -jnp.inf)
            top = jnp.max(scores, axis=0, keepdims=True)
            grown = jnp.exp2((scores - top) * (LOG2E / 8.0))
            probs = grown * (1.0 / jnp.sum(grown, axis=0, keepdims=True))
            probs_low = probs.astype(BF16)
            out = jnp.dot(bt[DH:], probs_low, preferred_element_type=F32).astype(BF16).astype(F32)
            delta = jnp.sum(out * at[DH:, part].astype(F32), axis=0, keepdims=True)
            prob_grads = jnp.dot(b, gt[:, part], preferred_element_type=F32)
            score_grads = (probs * (prob_grads - delta)).astype(BF16)
            dq = jnp.dot(bt[:DH], score_grads, preferred_element_type=F32) * 0.125
            first = jnp.concatenate([dq, out], axis=0).T.astype(BF16)
            dk = dk + jnp.dot(score_grads, a[part], preferred_element_type=F32)
            dv = dv + jnp.dot(probs_low, a[part], preferred_element_type=F32)
            if c * CHUNK < CHIP:
                res_own[t, 0, part] = first
            else:
                res_nb[t, 0, c * CHUNK - CHIP : (c + 1) * CHUNK - CHIP] = first
        second = jnp.where(low, dk * 0.125, dv).astype(BF16)
        res_own[t, 1] = second[:CHIP]
        res_nb[t, 1] = second[CHIP:]

    def receive(s):
        to_right(s, own.at[0]).wait_recv()
        to_left(s, own.at[0]).wait_recv()

    def settle(s):
        h = s - LAG
        for i in range(2):
            for rows, out in ((mine, fin), (theirs, fin_out)):
                at = home[rows]
                out[h, i] = jnp.where(
                    at > 0, recv_r[s, i, rows], jnp.where(at < 0, recv_l[s, i, rows], res_own[h, i, rows])
                )
        hand_back(h).start()

    def step(t, _):
        receive(t)
        attend(t)
        s = t + LAG

        @pl.when(s < HEADS)
        def _():
            exchange(s).wait_recv()
            at = home[...]
            for i in range(2):
                send_r[t, i] = jnp.where(at > 0, own[s, i], res_nb[t, i])
                send_l[t, i] = jnp.where(at < 0, own[s, i], res_nb[t, i])
            to_right(s, send_r.at[t]).start()
            to_left(s, send_l.at[t]).start()

        @pl.when(s >= HEADS)
        def _():
            to_right(s, res_nb.at[t]).start()
            to_left(s, res_nb.at[t]).start()

        @pl.when(t >= LAG)
        def _():
            settle(t)

        return 0

    lax.fori_loop(0, HEADS, step, 0)
    for s in range(HEADS, SLOTS):
        receive(s)
        settle(s)

    def unpack(source, pair, place):
        lanes = pl.ds(pl.multiple_of(place * 2 * DH, 2 * DH), 2 * DH)
        e, o = 2 * pair, 2 * pair + 1
        dq_ref[:, lanes] = join(source[e, 0], source[o, 0], 0)
        o_ref[:, lanes] = join(source[e, 0], source[o, 0], 1)
        dk_ref[:, lanes] = join(source[e, 1], source[o, 1], 0)
        dv_ref[:, lanes] = join(source[e, 1], source[o, 1], 1)

    def unpack_mine(pair, _):
        unpack(fin, pair, core * (HEADS // 2) + pair)
        return 0

    def unpack_theirs(pair, _):
        hand_back(2 * pair).wait_recv()
        hand_back(2 * pair + 1).wait_recv()
        unpack(fin_in, pair, (1 - core) * (HEADS // 2) + pair)
        return 0

    lax.fori_loop(0, HEADS // 2, unpack_mine, 0)
    lax.fori_loop(0, HEADS // 2, unpack_theirs, 0)

    def drain(h, _):
        exchange(h).wait_send()
        hand_back(h).wait_send()
        return 0

    def drain_slots(s, _):
        to_right(s, own.at[0]).wait_send()
        to_left(s, own.at[0]).wait_send()
        return 0

    lax.fori_loop(0, HEADS, drain, 0)
    lax.fori_loop(0, SLOTS, drain_slots, 0)


def on_device(queries, keys, values, cotangent, doc_lengths):
    n = lax.axis_size("ctx")
    block = (2, CHIP, 2 * DH)
    half = (2, ROWS, 2 * DH)
    whole = pl.BlockSpec(memory_space=pltpu.VMEM)
    pairs = 2 * CHIP * 2 * CHIP * HEADS
    return pl.pallas_call(
        functools.partial(kernel, n),
        out_shape=[jax.ShapeDtypeStruct(queries.shape, BF16)] * 4,
        in_specs=[whole] * 5,
        out_specs=[whole] * 4,
        scratch_shapes=[
            pltpu.VMEM((HEADS, *block), BF16),
            pltpu.VMEM((HEADS, *half), BF16),
            pltpu.VMEM((HEADS, *block), BF16),
            pltpu.VMEM((HEADS, *block), BF16),
            pltpu.VMEM((HEADS - LAG, *block), BF16),
            pltpu.VMEM((HEADS - LAG, *block), BF16),
            pltpu.VMEM((SLOTS, *block), BF16),
            pltpu.VMEM((SLOTS, *block), BF16),
            pltpu.VMEM((HEADS, *half), BF16),
            pltpu.VMEM((HEADS, *half), BF16),
            pltpu.VMEM((HEADS, *half), BF16),
            pltpu.VMEM((1, 2 * CHIP), F32),
            pltpu.VMEM((2 * CHIP, 128), F32),
            pltpu.VMEM((CHIP, 128), BF16),
            pltpu.VMEM((CHIP, 128), BF16),
            pltpu.SemaphoreType.DMA((HEADS,)),
            pltpu.SemaphoreType.DMA((HEADS,)),
            pltpu.SemaphoreType.DMA((SLOTS,)),
            pltpu.SemaphoreType.DMA((SLOTS,)),
            pltpu.SemaphoreType.DMA((SLOTS,)),
            pltpu.SemaphoreType.DMA((SLOTS,)),
            pltpu.SemaphoreType.DMA((HEADS,)),
            pltpu.SemaphoreType.DMA((HEADS,)),
        ],
        compiler_params=pltpu.CompilerParams(
            collective_id=0, has_side_effects=True, vmem_limit_bytes=40 * 1024 * 1024
        ),
        cost_estimate=pl.CostEstimate(flops=12 * DH * pairs, bytes_accessed=1 << 21, transcendentals=pairs),
    )(doc_lengths.reshape(1, -1), queries, keys, values, cotangent)


def solution(mesh):
    rows = P(("dp", "ctx"), None)
    return jax.shard_map(
        on_device,
        mesh=mesh,
        in_specs=(rows, rows, rows, rows, P("dp")),
        out_specs=(rows, rows, rows, rows),
        check_vma=False,
    )
```

```python
import functools

import jax
import jax.numpy as jnp
from jax import lax
from jax.experimental import pallas as pl
from jax.experimental.pallas import tpu as pltpu
from jax.sharding import PartitionSpec as P

H = 16
DH = 64
ROWS = 128
CHIP = 2 * ROWS
HEADS = H // 2
LAG = 3
SLOTS = HEADS + LAG
VMEM_LIMIT = 40 * 1024 * 1024
LOG2E = 1.4426950408889634
F32 = jnp.float32
BF16 = jnp.bfloat16


def low_lanes(shape):
    return lax.broadcasted_iota(jnp.int32, shape, 1) < DH


def join(left, right, half):
    lanes = slice(0, DH) if half == 0 else slice(DH, 2 * DH)
    return jnp.concatenate([left[:, lanes], right[:, lanes]], axis=1)


def token_info(ends, base, axis, total):
    shape = (CHIP, 1) if axis == 0 else (1, CHIP)
    place = lax.broadcasted_iota(jnp.int32, shape, axis).astype(F32) + base
    before = ends <= place
    start = jnp.max(jnp.where(before, ends, 0.0), axis=1 - axis, keepdims=True)
    end = jnp.min(jnp.where(before, 4.0 * total, ends), axis=1 - axis, keepdims=True)
    first = jnp.floor(start * (1.0 / CHIP))
    last = jnp.floor((end - 1.0) * (1.0 / CHIP))
    owner = jnp.minimum(first + 1.0, last)
    inside = (place >= 0.0) & (place < total)
    return start, jnp.where(inside, owner, -9.0)


def kernel(
    n,
    len_hbm,
    q_hbm,
    k_hbm,
    v_hbm,
    g_hbm,
    o_ref,
    dq_ref,
    dk_ref,
    dv_ref,
    loaded,
    len_ref,
    own,
    stage,
    res_own,
    res_nb,
    send_r,
    send_l,
    recv_l,
    recv_r,
    fin,
    fin_out,
    fin_in,
    id_row,
    id_col,
    home,
    guest,
    load_sem,
    sib_send,
    sib_recv,
    r_send,
    r_recv,
    l_send,
    l_recv,
    cross_send,
    cross_recv,
    fin_send,
    fin_recv,
):
    me = lax.axis_index("ctx")
    core = lax.rem(me, 2)
    chip = lax.div(me, 2)
    sibling = me + 1 - 2 * core
    right = lax.rem(me + 2, n)
    left = lax.rem(me + n - 2, n)
    across = (lax.rem(sibling + 2, n), lax.rem(sibling + n - 2, n))
    mine = pl.ds(pl.multiple_of(core * ROWS, ROWS), ROWS)
    theirs = pl.ds(pl.multiple_of((1 - core) * ROWS, ROWS), ROWS)

    loads = [
        pltpu.make_async_copy(src, loaded.at[i], load_sem.at[i]) for i, src in enumerate((q_hbm, k_hbm, v_hbm, g_hbm))
    ]
    len_load = pltpu.make_async_copy(len_hbm, len_ref, load_sem.at[4])
    for load in (*loads, len_load):
        load.start()

    barrier = pltpu.get_barrier_semaphore()
    for other in (sibling, right, left, *across):
        pl.semaphore_signal(barrier, inc=1, device_id={"ctx": other}, device_id_type=pl.DeviceIdType.MESH)

    def remote(src, dst, send_sem, recv_sem, target):
        return pltpu.make_async_remote_copy(
            src_ref=src,
            dst_ref=dst,
            send_sem=send_sem,
            recv_sem=recv_sem,
            device_id={"ctx": target},
            device_id_type=pl.DeviceIdType.MESH,
        )

    def exchange(h):
        return remote(stage.at[h], own.at[h, :, mine], sib_send.at[h], sib_recv.at[h], sibling)

    def whole_slot(s, src_r, src_l):
        return (
            remote(src_r, recv_l.at[s], r_send.at[s], r_recv.at[s], right),
            remote(src_l, recv_r.at[s], l_send.at[s], l_recv.at[s], left),
        )

    def halved_slot(s, extra, straight, crossed):
        return (
            remote(straight, recv_l.at[s, :, mine], r_send.at[s], r_recv.at[s], right),
            remote(straight, recv_r.at[s, :, mine], l_send.at[s], l_recv.at[s], left),
            remote(crossed, recv_l.at[s, :, mine], cross_send.at[0, extra], cross_recv.at[0, extra], across[0]),
            remote(crossed, recv_r.at[s, :, mine], cross_send.at[1, extra], cross_recv.at[1, extra], across[1]),
        )

    def early_slot(s):
        return halved_slot(s, s, own.at[s, :, mine], stage.at[s])

    def late_slot(s):
        h = s - LAG
        return halved_slot(s, s - HEADS + LAG, res_nb.at[h, :, mine], res_nb.at[h, :, theirs])

    def hand_back(h):
        return remote(fin_out.at[h], fin_in.at[h], fin_send.at[h], fin_recv.at[h], sibling)

    def hand_raw(h):
        return remote(res_own.at[h, :, theirs], fin_in.at[h], fin_send.at[h], fin_recv.at[h], sibling)

    def packed(pair, half):
        lanes = pl.ds(pl.multiple_of(pair * 2 * DH, 2 * DH), 2 * DH)
        q, k, v, g = [loaded[i, :, lanes] for i in range(4)]
        return join(q, g, half), join(k, v, half)

    def pack(pair, _):
        for half in range(2):
            h = 2 * pair + half
            a, b = packed((1 - core) * (HEADS // 2) + pair, half)
            stage[h, 0] = a
            stage[h, 1] = b
            a, b = packed(core * (HEADS // 2) + pair, half)
            own[h, 0, mine] = a
            own[h, 1, mine] = b
        return 0

    for load in loads:
        load.wait()
    ready = (LAG + 1) // 2
    for pair in range(ready):
        pack(pair, 0)
    pl.semaphore_wait(barrier, 5)
    for s in range(LAG):
        for copy in early_slot(s):
            copy.start()
    for h in range(2 * ready):
        exchange(h).start()

    def pack_rest(pair, _):
        pack(pair, 0)
        exchange(2 * pair).start()
        exchange(2 * pair + 1).start()
        return 0

    lax.fori_loop(ready, HEADS // 2, pack_rest, 0)

    len_load.wait()
    here = chip.astype(F32)
    total = float(n * ROWS)
    docs = len_ref.shape[1]
    over = lax.broadcasted_iota(jnp.int32, (docs, docs), 1)
    down = lax.broadcasted_iota(jnp.int32, (docs, docs), 0)
    lengths = jnp.broadcast_to(len_ref[...].astype(F32), (docs, docs))
    ends_col = jnp.sum(jnp.where(over <= down, lengths, 0.0), axis=1, keepdims=True)
    ends_row = jnp.sum(jnp.where(over == down, ends_col, 0.0), axis=0, keepdims=True)
    for axis, ends in ((1, ends_col), (0, ends_row)):
        start_o, owner_o = token_info(ends, here * CHIP, axis, total)
        start_l, owner_l = token_info(ends, (here - 1.0) * CHIP, axis, total)
        start_r, owner_r = token_info(ends, (here + 1.0) * CHIP, axis, total)
        id_own = jnp.where(owner_o == here, start_o, -1.0)
        id_nb = jnp.where(owner_l == here, start_l, jnp.where(owner_r == here, start_r, -2.0))
        if axis == 1:
            id_row[:, 0:CHIP] = id_own
            id_row[:, CHIP:] = id_nb
        else:
            id_col[0:CHIP] = jnp.broadcast_to(id_own, (CHIP, 128))
            id_col[CHIP:] = jnp.broadcast_to(id_nb, (CHIP, 128))
            home[...] = jnp.broadcast_to(owner_o - here, (CHIP, 128)).astype(BF16)
            came = jnp.where(owner_l == here, -1.0, jnp.where(owner_r == here, 1.0, 0.0))
            guest[...] = jnp.broadcast_to(came, (CHIP, 128)).astype(BF16)

    def attend(t):
        came = guest[...]
        zero = jnp.zeros((CHIP, 2 * DH), BF16)
        both = []
        for i in range(2):
            nb = jnp.where(came < 0, recv_l[t, i], jnp.where(came > 0, recv_r[t, i], zero))
            both.append(jnp.concatenate([own[t, i], nb], axis=0))
        a, b = both
        at = a.T
        bt = b.T
        none = jnp.zeros((DH, 2 * CHIP), BF16)
        qt = jnp.concatenate([at[:DH], none], axis=0)
        gt = jnp.concatenate([none, at[DH:]], axis=0)
        ids = jnp.concatenate([id_col[...]] * (2 * CHIP // 128), axis=1)
        scores = jnp.dot(b, qt, preferred_element_type=F32)
        scores = jnp.where(ids == id_row[...], scores, -jnp.inf)
        top = jnp.max(scores, axis=0, keepdims=True)
        grown = jnp.exp2((scores - top) * (LOG2E / 8.0))
        probs = grown * (1.0 / jnp.sum(grown, axis=0, keepdims=True))
        probs_low = probs.astype(BF16)
        out = jnp.dot(bt[DH:], probs_low, preferred_element_type=F32).astype(BF16).astype(F32)
        delta = jnp.sum(out * at[DH:].astype(F32), axis=0, keepdims=True)
        prob_grads = jnp.dot(b, gt, preferred_element_type=F32)
        score_grads = (probs * (prob_grads - delta)).astype(BF16)
        dq = jnp.dot(bt[:DH], score_grads, preferred_element_type=F32) * 0.125
        first = jnp.concatenate([dq, out], axis=0).T.astype(BF16)
        dk = jnp.dot(score_grads, a, preferred_element_type=F32) * 0.125
        dv = jnp.dot(probs_low, a, preferred_element_type=F32)
        second = jnp.where(low_lanes((2 * CHIP, 2 * DH)), dk, dv).astype(BF16)
        for i, result in enumerate((first, second)):
            res_own[t, i] = result[:CHIP]
            res_nb[t, i] = result[CHIP:]

    def settle(h, at, rows, mid, out):
        for i in range(2):
            out[h, i] = jnp.where(
                at > 0, recv_r[h + LAG, i, rows], jnp.where(at < 0, recv_l[h + LAG, i, rows], mid[i])
            )

    def step(t, _):
        @pl.when(t < LAG)
        def _():
            for copy in early_slot(t):
                copy.wait_recv()
            exchange(t).wait_recv()

        @pl.when(t >= LAG)
        def _():
            for copy in whole_slot(t, own.at[0], own.at[0]):
                copy.wait_recv()

        attend(t)
        s = t + LAG

        @pl.when(s < HEADS)
        def _():
            exchange(s).wait_recv()
            at = home[...]
            for i in range(2):
                send_r[t, i] = jnp.where(at > 0, own[s, i], res_nb[t, i])
                send_l[t, i] = jnp.where(at < 0, own[s, i], res_nb[t, i])
            for copy in whole_slot(s, send_r.at[t], send_l.at[t]):
                copy.start()

        @pl.when(s >= HEADS)
        def _():
            for copy in late_slot(s):
                copy.start()
            hand_raw(t).start()

        @pl.when(t >= LAG)
        def _():
            h = t - LAG
            settle(h, home[theirs], theirs, res_own.at[h, :, theirs], fin_out)
            hand_back(h).start()
            settle(h, home[mine], mine, res_own.at[h, :, mine], fin)

        return 0

    lax.fori_loop(0, HEADS, step, 0)

    def unpack(source, pair, place):
        lanes = pl.ds(pl.multiple_of(place * 2 * DH, 2 * DH), 2 * DH)
        e, o = 2 * pair, 2 * pair + 1
        dq_ref[:, lanes] = join(source[e, 0], source[o, 0], 0)
        o_ref[:, lanes] = join(source[e, 0], source[o, 0], 1)
        dk_ref[:, lanes] = join(source[e, 1], source[o, 1], 0)
        dv_ref[:, lanes] = join(source[e, 1], source[o, 1], 1)

    def unpack_both(pair, _):
        unpack(fin, pair, core * (HEADS // 2) + pair)
        unpack(fin_in, pair, (1 - core) * (HEADS // 2) + pair)
        return 0

    def handed(h, _):
        hand_back(h).wait_recv()
        return 0

    lax.fori_loop(0, HEADS, handed, 0)
    settled = (HEADS - LAG) // 2
    lax.fori_loop(0, settled, unpack_both, 0)
    at = home[mine]
    for s in range(HEADS, SLOTS):
        h = s - LAG
        for copy in late_slot(s):
            copy.wait_recv()
        settle(h, at, mine, res_own.at[h, :, mine], fin)
        settle(h, at, theirs, fin_in.at[h], fin_in)
        if h % 2:
            unpack_both(h // 2, 0)

    def drain(h, _):
        exchange(h).wait_send()
        hand_back(h).wait_send()
        return 0

    def drain_slots(s, _):
        for copy in whole_slot(s, own.at[0], own.at[0]):
            copy.wait_send()
        return 0

    lax.fori_loop(0, HEADS, drain, 0)
    lax.fori_loop(LAG, HEADS, drain_slots, 0)
    for s in range(LAG):
        for copy in (*early_slot(s), *late_slot(HEADS + s)):
            copy.wait_send()


def write_out(*refs):
    sources, outs, sems = refs[:4], refs[4:8], refs[8]
    copies = [pltpu.make_async_copy(src, dst, sems.at[i]) for i, (src, dst) in enumerate(zip(sources, outs))]
    for copy in copies:
        copy.start()
    for copy in copies:
        copy.wait()


def on_device(queries, keys, values, cotangent, doc_lengths):
    n = lax.axis_size("ctx")
    block = (2, CHIP, 2 * DH)
    half = (2, ROWS, 2 * DH)
    vmem = pl.BlockSpec(memory_space=pltpu.VMEM)
    anywhere = pl.BlockSpec(memory_space=pl.ANY)
    pairs = 2 * CHIP * 2 * CHIP * HEADS
    outs = [jax.ShapeDtypeStruct(queries.shape, BF16)] * 4
    dma = pltpu.SemaphoreType.DMA
    queries, keys, values, cotangent, lengths = [
        pltpu.with_memory_space_constraint(x, pltpu.HBM)
        for x in (queries, keys, values, cotangent, doc_lengths.reshape(1, -1))
    ]
    results = pl.pallas_call(
        functools.partial(kernel, n),
        out_shape=[pltpu.VMEM(queries.shape, BF16)] * 4,
        in_specs=[anywhere] * 5,
        out_specs=[vmem] * 4,
        scratch_shapes=[
            pltpu.VMEM((4, *queries.shape), BF16),
            pltpu.VMEM((1, doc_lengths.shape[0]), jnp.int32),
            pltpu.VMEM((HEADS, *block), BF16),
            pltpu.VMEM((HEADS, *half), BF16),
            pltpu.VMEM((HEADS, *block), BF16),
            pltpu.VMEM((HEADS, *block), BF16),
            pltpu.VMEM((HEADS - LAG, *block), BF16),
            pltpu.VMEM((HEADS - LAG, *block), BF16),
            pltpu.VMEM((SLOTS, *block), BF16),
            pltpu.VMEM((SLOTS, *block), BF16),
            pltpu.VMEM((HEADS, *half), BF16),
            pltpu.VMEM((HEADS, *half), BF16),
            pltpu.VMEM((HEADS, *half), BF16),
            pltpu.VMEM((1, 2 * CHIP), F32),
            pltpu.VMEM((2 * CHIP, 128), F32),
            pltpu.VMEM((CHIP, 128), BF16),
            pltpu.VMEM((CHIP, 128), BF16),
            dma((5,)),
            dma((HEADS,)),
            dma((HEADS,)),
            dma((SLOTS,)),
            dma((SLOTS,)),
            dma((SLOTS,)),
            dma((SLOTS,)),
            dma((2, 2 * LAG)),
            dma((2, 2 * LAG)),
            dma((HEADS,)),
            dma((HEADS,)),
        ],
        compiler_params=pltpu.CompilerParams(
            collective_id=0, has_side_effects=True, vmem_limit_bytes=VMEM_LIMIT
        ),
        cost_estimate=pl.CostEstimate(flops=12 * DH * pairs, bytes_accessed=1 << 21, transcendentals=pairs),
    )(lengths, queries, keys, values, cotangent)
    return tuple(
        pl.pallas_call(
            write_out,
            out_shape=outs,
            in_specs=[vmem] * 4,
            out_specs=[anywhere] * 4,
            scratch_shapes=[dma((4,))],
            compiler_params=pltpu.CompilerParams(vmem_limit_bytes=16 * 1024 * 1024),
        )(*results)
    )


def solution(mesh):
    rows = P(("dp", "ctx"), None)
    return jax.shard_map(
        on_device,
        mesh=mesh,
        in_specs=(rows, rows, rows, rows, P("dp")),
        out_specs=(rows, rows, rows, rows),
        check_vma=False,
    )
```

```python
import functools

import jax
import jax.numpy as jnp
from jax import lax
from jax.experimental import pallas as pl
from jax.experimental.pallas import tpu as pltpu
from jax.sharding import PartitionSpec as P

H = 16
DH = 64
ROWS = 128
CHIP = 2 * ROWS
HEADS = H // 2
LAG = 3
SLOTS = HEADS + LAG
VMEM_LIMIT = 40 * 1024 * 1024
LOG2E = 1.4426950408889634
F32 = jnp.float32
BF16 = jnp.bfloat16


def low_lanes(shape):
    return lax.broadcasted_iota(jnp.int32, shape, 1) < DH


def join(left, right, half):
    lanes = slice(0, DH) if half == 0 else slice(DH, 2 * DH)
    return jnp.concatenate([left[:, lanes], right[:, lanes]], axis=1)


def token_info(ends, base, axis, total):
    shape = (CHIP, 1) if axis == 0 else (1, CHIP)
    place = lax.broadcasted_iota(jnp.int32, shape, axis).astype(F32) + base
    before = ends <= place
    start = jnp.max(jnp.where(before, ends, 0.0), axis=1 - axis, keepdims=True)
    end = jnp.min(jnp.where(before, 4.0 * total, ends), axis=1 - axis, keepdims=True)
    first = jnp.floor(start * (1.0 / CHIP))
    last = jnp.floor((end - 1.0) * (1.0 / CHIP))
    owner = jnp.minimum(first + 1.0, last)
    inside = (place >= 0.0) & (place < total)
    return start, jnp.where(inside, owner, -9.0)


def kernel(
    n,
    len_hbm,
    q_hbm,
    k_hbm,
    v_hbm,
    g_hbm,
    o_ref,
    dq_ref,
    dk_ref,
    dv_ref,
    loaded,
    len_ref,
    own,
    stage,
    res_own,
    res_nb,
    send_r,
    send_l,
    recv_l,
    recv_r,
    fin,
    fin_out,
    fin_in,
    id_row,
    id_col,
    home,
    guest,
    load_sem,
    sib_send,
    sib_recv,
    r_send,
    r_recv,
    l_send,
    l_recv,
    cross_send,
    cross_recv,
    fin_send,
    fin_recv,
):
    me = lax.axis_index("ctx")
    core = lax.rem(me, 2)
    chip = lax.div(me, 2)
    sibling = me + 1 - 2 * core
    right = lax.rem(me + 2, n)
    left = lax.rem(me + n - 2, n)
    across = (lax.rem(sibling + 2, n), lax.rem(sibling + n - 2, n))
    mine = pl.ds(pl.multiple_of(core * ROWS, ROWS), ROWS)
    theirs = pl.ds(pl.multiple_of((1 - core) * ROWS, ROWS), ROWS)

    loads = [
        pltpu.make_async_copy(src, loaded.at[i], load_sem.at[i]) for i, src in enumerate((q_hbm, k_hbm, v_hbm, g_hbm))
    ]
    len_load = pltpu.make_async_copy(len_hbm, len_ref, load_sem.at[4])
    for load in (*loads, len_load):
        load.start()

    has_left = chip > 0
    has_right = chip < n // 2 - 1
    barrier = pltpu.get_barrier_semaphore()

    def greet(others):
        for other in others:
            pl.semaphore_signal(barrier, inc=1, device_id={"ctx": other}, device_id_type=pl.DeviceIdType.MESH)

    greet((sibling,))
    pl.when(has_right)(lambda: greet((right, across[0])))
    pl.when(has_left)(lambda: greet((left, across[1])))

    def remote(src, dst, send_sem, recv_sem, target):
        return pltpu.make_async_remote_copy(
            src_ref=src,
            dst_ref=dst,
            send_sem=send_sem,
            recv_sem=recv_sem,
            device_id={"ctx": target},
            device_id_type=pl.DeviceIdType.MESH,
        )

    def exchange(h):
        return remote(stage.at[h], own.at[h, :, mine], sib_send.at[h], sib_recv.at[h], sibling)

    def whole_slot(s, src_r, src_l):
        return (
            (remote(src_r, recv_l.at[s], r_send.at[s], r_recv.at[s], right),),
            (remote(src_l, recv_r.at[s], l_send.at[s], l_recv.at[s], left),),
        )

    def halved_slot(s, extra, straight, crossed):
        return (
            (
                remote(straight, recv_l.at[s, :, mine], r_send.at[s], r_recv.at[s], right),
                remote(crossed, recv_l.at[s, :, mine], cross_send.at[0, extra], cross_recv.at[0, extra], across[0]),
            ),
            (
                remote(straight, recv_r.at[s, :, mine], l_send.at[s], l_recv.at[s], left),
                remote(crossed, recv_r.at[s, :, mine], cross_send.at[1, extra], cross_recv.at[1, extra], across[1]),
            ),
        )

    def launch(slot):
        pl.when(has_right)(lambda: [copy.start() for copy in slot[0]] and None)
        pl.when(has_left)(lambda: [copy.start() for copy in slot[1]] and None)

    def sent(slot):
        pl.when(has_right)(lambda: [copy.wait_send() for copy in slot[0]] and None)
        pl.when(has_left)(lambda: [copy.wait_send() for copy in slot[1]] and None)

    def arrived(slot):
        pl.when(has_left)(lambda: [copy.wait_recv() for copy in slot[0]] and None)
        pl.when(has_right)(lambda: [copy.wait_recv() for copy in slot[1]] and None)

    def early_slot(s):
        return halved_slot(s, s, own.at[s, :, mine], stage.at[s])

    def late_slot(s):
        h = s - LAG
        return halved_slot(s, s - HEADS + LAG, res_nb.at[h, :, mine], res_nb.at[h, :, theirs])

    def hand_back(h):
        return remote(fin_out.at[h], fin_in.at[h], fin_send.at[h], fin_recv.at[h], sibling)

    def hand_raw(h):
        return remote(res_own.at[h, :, theirs], fin_in.at[h], fin_send.at[h], fin_recv.at[h], sibling)

    def packed(pair, half):
        lanes = pl.ds(pl.multiple_of(pair * 2 * DH, 2 * DH), 2 * DH)
        q, k, v, g = [loaded[i, :, lanes] for i in range(4)]
        return join(q, g, half), join(k, v, half)

    def pack(pair, _):
        for half in range(2):
            h = 2 * pair + half
            a, b = packed((1 - core) * (HEADS // 2) + pair, half)
            stage[h, 0] = a
            stage[h, 1] = b
            a, b = packed(core * (HEADS // 2) + pair, half)
            own[h, 0, mine] = a
            own[h, 1, mine] = b
        return 0

    for load in loads:
        load.wait()
    ready = (LAG + 1) // 2
    for pair in range(ready):
        pack(pair, 0)
    pl.semaphore_wait(barrier, 1 + 2 * has_left.astype(jnp.int32) + 2 * has_right.astype(jnp.int32))
    for s in range(LAG):
        launch(early_slot(s))
    for h in range(2 * ready):
        exchange(h).start()

    def pack_rest(pair, _):
        pack(pair, 0)
        exchange(2 * pair).start()
        exchange(2 * pair + 1).start()
        return 0

    lax.fori_loop(ready, HEADS // 2, pack_rest, 0)

    len_load.wait()
    here = chip.astype(F32)
    total = float(n * ROWS)
    docs = len_ref.shape[1]
    over = lax.broadcasted_iota(jnp.int32, (docs, docs), 1)
    down = lax.broadcasted_iota(jnp.int32, (docs, docs), 0)
    lengths = jnp.broadcast_to(len_ref[...].astype(F32), (docs, docs))
    ends_col = jnp.sum(jnp.where(over <= down, lengths, 0.0), axis=1, keepdims=True)
    ends_row = jnp.sum(jnp.where(over == down, ends_col, 0.0), axis=0, keepdims=True)
    for axis, ends in ((1, ends_col), (0, ends_row)):
        start_o, owner_o = token_info(ends, here * CHIP, axis, total)
        start_l, owner_l = token_info(ends, (here - 1.0) * CHIP, axis, total)
        start_r, owner_r = token_info(ends, (here + 1.0) * CHIP, axis, total)
        id_own = jnp.where(owner_o == here, start_o, -1.0)
        id_nb = jnp.where(owner_l == here, start_l, jnp.where(owner_r == here, start_r, -2.0))
        if axis == 1:
            id_row[:, 0:CHIP] = id_own
            id_row[:, CHIP:] = id_nb
        else:
            id_col[0:CHIP] = jnp.broadcast_to(id_own, (CHIP, 128))
            id_col[CHIP:] = jnp.broadcast_to(id_nb, (CHIP, 128))
            home[...] = jnp.broadcast_to(owner_o - here, (CHIP, 128)).astype(BF16)
            came = jnp.where(owner_l == here, -1.0, jnp.where(owner_r == here, 1.0, 0.0))
            guest[...] = jnp.broadcast_to(came, (CHIP, 128)).astype(BF16)

    def attend(t):
        came = guest[...]
        zero = jnp.zeros((CHIP, 2 * DH), BF16)
        both = []
        for i in range(2):
            nb = jnp.where(came < 0, recv_l[t, i], jnp.where(came > 0, recv_r[t, i], zero))
            both.append(jnp.concatenate([own[t, i], nb], axis=0))
        a, b = both
        at = a.T
        bt = b.T
        none = jnp.zeros((DH, 2 * CHIP), BF16)
        qt = jnp.concatenate([at[:DH], none], axis=0)
        gt = jnp.concatenate([none, at[DH:]], axis=0)
        ids = jnp.concatenate([id_col[...]] * (2 * CHIP // 128), axis=1)
        scores = jnp.dot(b, qt, preferred_element_type=F32)
        scores = jnp.where(ids == id_row[...], scores, -jnp.inf)
        top = jnp.max(scores, axis=0, keepdims=True)
        grown = jnp.exp2((scores - top) * (LOG2E / 8.0))
        probs = grown * (1.0 / jnp.sum(grown, axis=0, keepdims=True))
        probs_low = probs.astype(BF16)
        out = jnp.dot(bt[DH:], probs_low, preferred_element_type=F32).astype(BF16).astype(F32)
        delta = jnp.sum(out * at[DH:].astype(F32), axis=0, keepdims=True)
        prob_grads = jnp.dot(b, gt, preferred_element_type=F32)
        score_grads = (probs * (prob_grads - delta)).astype(BF16)
        dq = jnp.dot(bt[:DH], score_grads, preferred_element_type=F32) * 0.125
        first = jnp.concatenate([dq, out], axis=0).T.astype(BF16)
        dk = jnp.dot(score_grads, a, preferred_element_type=F32) * 0.125
        dv = jnp.dot(probs_low, a, preferred_element_type=F32)
        second = jnp.where(low_lanes((2 * CHIP, 2 * DH)), dk, dv).astype(BF16)
        for i, result in enumerate((first, second)):
            res_own[t, i] = result[:CHIP]
            res_nb[t, i] = result[CHIP:]

    def settle(h, at, rows, mid, out):
        for i in range(2):
            out[h, i] = jnp.where(
                at > 0, recv_r[h + LAG, i, rows], jnp.where(at < 0, recv_l[h + LAG, i, rows], mid[i])
            )

    def step(t, _):
        @pl.when(t < LAG)
        def _():
            arrived(early_slot(t))
            exchange(t).wait_recv()

        @pl.when(t >= LAG)
        def _():
            arrived(whole_slot(t, own.at[0], own.at[0]))

        attend(t)
        s = t + LAG

        @pl.when(s < HEADS)
        def _():
            exchange(s).wait_recv()
            at = home[...]
            for i in range(2):
                send_r[t, i] = jnp.where(at > 0, own[s, i], res_nb[t, i])
                send_l[t, i] = jnp.where(at < 0, own[s, i], res_nb[t, i])
            launch(whole_slot(s, send_r.at[t], send_l.at[t]))

        @pl.when(s >= HEADS)
        def _():
            launch(late_slot(s))
            hand_raw(t).start()

        @pl.when(t >= LAG)
        def _():
            h = t - LAG
            settle(h, home[theirs], theirs, res_own.at[h, :, theirs], fin_out)
            hand_back(h).start()
            settle(h, home[mine], mine, res_own.at[h, :, mine], fin)

        return 0

    lax.fori_loop(0, HEADS, step, 0)

    def unpack(source, pair, place):
        lanes = pl.ds(pl.multiple_of(place * 2 * DH, 2 * DH), 2 * DH)
        e, o = 2 * pair, 2 * pair + 1
        dq_ref[:, lanes] = join(source[e, 0], source[o, 0], 0)
        o_ref[:, lanes] = join(source[e, 0], source[o, 0], 1)
        dk_ref[:, lanes] = join(source[e, 1], source[o, 1], 0)
        dv_ref[:, lanes] = join(source[e, 1], source[o, 1], 1)

    def unpack_both(pair, _):
        unpack(fin, pair, core * (HEADS // 2) + pair)
        unpack(fin_in, pair, (1 - core) * (HEADS // 2) + pair)
        return 0

    def handed(h, _):
        hand_back(h).wait_recv()
        return 0

    lax.fori_loop(0, HEADS, handed, 0)
    settled = (HEADS - LAG) // 2
    lax.fori_loop(0, settled, unpack_both, 0)
    at = home[mine]
    for s in range(HEADS, SLOTS):
        h = s - LAG
        arrived(late_slot(s))
        settle(h, at, mine, res_own.at[h, :, mine], fin)
        settle(h, at, theirs, fin_in.at[h], fin_in)
        if h % 2:
            unpack_both(h // 2, 0)

    def drain(h, _):
        exchange(h).wait_send()
        hand_back(h).wait_send()
        return 0

    def drain_slots(s, _):
        sent(whole_slot(s, own.at[0], own.at[0]))
        return 0

    lax.fori_loop(0, HEADS, drain, 0)
    lax.fori_loop(LAG, HEADS, drain_slots, 0)
    for s in range(LAG):
        sent(early_slot(s))
        sent(late_slot(HEADS + s))


def write_out(*refs):
    sources, outs, sems = refs[:4], refs[4:8], refs[8]
    copies = [pltpu.make_async_copy(src, dst, sems.at[i]) for i, (src, dst) in enumerate(zip(sources, outs))]
    for copy in copies:
        copy.start()
    for copy in copies:
        copy.wait()


def on_device(queries, keys, values, cotangent, doc_lengths):
    n = lax.axis_size("ctx")
    block = (2, CHIP, 2 * DH)
    half = (2, ROWS, 2 * DH)
    vmem = pl.BlockSpec(memory_space=pltpu.VMEM)
    anywhere = pl.BlockSpec(memory_space=pl.ANY)
    pairs = 2 * CHIP * 2 * CHIP * HEADS
    outs = [jax.ShapeDtypeStruct(queries.shape, BF16)] * 4
    dma = pltpu.SemaphoreType.DMA
    queries, keys, values, cotangent, lengths = [
        pltpu.with_memory_space_constraint(x, pltpu.HBM)
        for x in (queries, keys, values, cotangent, doc_lengths.reshape(1, -1))
    ]
    results = pl.pallas_call(
        functools.partial(kernel, n),
        out_shape=[pltpu.VMEM(queries.shape, BF16)] * 4,
        in_specs=[anywhere] * 5,
        out_specs=[vmem] * 4,
        scratch_shapes=[
            pltpu.VMEM((4, *queries.shape), BF16),
            pltpu.VMEM((1, doc_lengths.shape[0]), jnp.int32),
            pltpu.VMEM((HEADS, *block), BF16),
            pltpu.VMEM((HEADS, *half), BF16),
            pltpu.VMEM((HEADS, *block), BF16),
            pltpu.VMEM((HEADS, *block), BF16),
            pltpu.VMEM((HEADS - LAG, *block), BF16),
            pltpu.VMEM((HEADS - LAG, *block), BF16),
            pltpu.VMEM((SLOTS, *block), BF16),
            pltpu.VMEM((SLOTS, *block), BF16),
            pltpu.VMEM((HEADS, *half), BF16),
            pltpu.VMEM((HEADS, *half), BF16),
            pltpu.VMEM((HEADS, *half), BF16),
            pltpu.VMEM((1, 2 * CHIP), F32),
            pltpu.VMEM((2 * CHIP, 128), F32),
            pltpu.VMEM((CHIP, 128), BF16),
            pltpu.VMEM((CHIP, 128), BF16),
            dma((5,)),
            dma((HEADS,)),
            dma((HEADS,)),
            dma((SLOTS,)),
            dma((SLOTS,)),
            dma((SLOTS,)),
            dma((SLOTS,)),
            dma((2, 2 * LAG)),
            dma((2, 2 * LAG)),
            dma((HEADS,)),
            dma((HEADS,)),
        ],
        compiler_params=pltpu.CompilerParams(
            collective_id=0, has_side_effects=True, vmem_limit_bytes=VMEM_LIMIT
        ),
        cost_estimate=pl.CostEstimate(flops=12 * DH * pairs, bytes_accessed=1 << 21, transcendentals=pairs),
    )(lengths, queries, keys, values, cotangent)
    return tuple(
        pl.pallas_call(
            write_out,
            out_shape=outs,
            in_specs=[vmem] * 4,
            out_specs=[anywhere] * 4,
            scratch_shapes=[dma((4,))],
            compiler_params=pltpu.CompilerParams(vmem_limit_bytes=16 * 1024 * 1024),
        )(*results)
    )


def solution(mesh):
    rows = P(("dp", "ctx"), None)
    return jax.shard_map(
        on_device,
        mesh=mesh,
        in_specs=(rows, rows, rows, rows, P("dp")),
        out_specs=(rows, rows, rows, rows),
        check_vma=False,
    )
```

```python
import functools

import jax
import jax.numpy as jnp
from jax import lax
from jax.experimental import pallas as pl
from jax.experimental.pallas import tpu as pltpu
from jax.sharding import PartitionSpec as P

H = 16
DH = 64
ROWS = 128
CHIP = 2 * ROWS
HEADS = H // 2
LAG = 3
SLOTS = HEADS + LAG
VMEM_LIMIT = 40 * 1024 * 1024
LOG2E = 1.4426950408889634
F32 = jnp.float32
BF16 = jnp.bfloat16


def low_lanes(shape):
    return lax.broadcasted_iota(jnp.int32, shape, 1) < DH


def join(left, right, half):
    lanes = slice(0, DH) if half == 0 else slice(DH, 2 * DH)
    return jnp.concatenate([left[:, lanes], right[:, lanes]], axis=1)


def token_info(ends, base, axis, total):
    shape = (CHIP, 1) if axis == 0 else (1, CHIP)
    place = lax.broadcasted_iota(jnp.int32, shape, axis).astype(F32) + base
    before = ends <= place
    start = jnp.max(jnp.where(before, ends, 0.0), axis=1 - axis, keepdims=True)
    end = jnp.min(jnp.where(before, 4.0 * total, ends), axis=1 - axis, keepdims=True)
    first = jnp.floor(start * (1.0 / CHIP))
    last = jnp.floor((end - 1.0) * (1.0 / CHIP))
    owner = jnp.minimum(first + 1.0, last)
    inside = (place >= 0.0) & (place < total)
    return start, jnp.where(inside, owner, -9.0)


def kernel(
    n,
    len_hbm,
    q_hbm,
    k_hbm,
    v_hbm,
    g_hbm,
    o_ref,
    dq_ref,
    dk_ref,
    dv_ref,
    loaded,
    len_ref,
    own,
    stage,
    res_own,
    res_nb,
    send_r,
    send_l,
    recv_l,
    recv_r,
    fin,
    fin_out,
    fin_in,
    id_row,
    id_col,
    home,
    guest,
    load_sem,
    sib_send,
    sib_recv,
    r_send,
    r_recv,
    l_send,
    l_recv,
    cross_send,
    cross_recv,
    fin_send,
    fin_recv,
):
    me = lax.axis_index("ctx")
    core = lax.rem(me, 2)
    chip = lax.div(me, 2)
    sibling = me + 1 - 2 * core
    right = lax.rem(me + 2, n)
    left = lax.rem(me + n - 2, n)
    across = (lax.rem(sibling + 2, n), lax.rem(sibling + n - 2, n))
    mine = pl.ds(pl.multiple_of(core * ROWS, ROWS), ROWS)
    theirs = pl.ds(pl.multiple_of((1 - core) * ROWS, ROWS), ROWS)

    has_left = chip > 0
    has_right = chip < n // 2 - 1
    barrier = pltpu.get_barrier_semaphore()

    def greet(others):
        for other in others:
            pl.semaphore_signal(barrier, inc=1, device_id={"ctx": other}, device_id_type=pl.DeviceIdType.MESH)

    greet((sibling,))
    pl.when(has_right)(lambda: greet((right, across[0])))
    pl.when(has_left)(lambda: greet((left, across[1])))

    loads = [
        pltpu.make_async_copy(src, loaded.at[i], load_sem.at[i]) for i, src in enumerate((q_hbm, k_hbm, v_hbm, g_hbm))
    ]
    len_load = pltpu.make_async_copy(len_hbm, len_ref, load_sem.at[4])
    for load in (*loads, len_load):
        load.start()

    def remote(src, dst, send_sem, recv_sem, target):
        return pltpu.make_async_remote_copy(
            src_ref=src,
            dst_ref=dst,
            send_sem=send_sem,
            recv_sem=recv_sem,
            device_id={"ctx": target},
            device_id_type=pl.DeviceIdType.MESH,
        )

    def exchange(h):
        return remote(stage.at[h], own.at[h, :, mine], sib_send.at[h], sib_recv.at[h], sibling)

    def whole_slot(s, src_r, src_l):
        return (
            (remote(src_r, recv_l.at[s], r_send.at[s], r_recv.at[s], right),),
            (remote(src_l, recv_r.at[s], l_send.at[s], l_recv.at[s], left),),
        )

    def halved_slot(s, extra, straight, crossed):
        return (
            (
                remote(straight, recv_l.at[s, :, mine], r_send.at[s], r_recv.at[s], right),
                remote(crossed, recv_l.at[s, :, mine], cross_send.at[0, extra], cross_recv.at[0, extra], across[0]),
            ),
            (
                remote(straight, recv_r.at[s, :, mine], l_send.at[s], l_recv.at[s], left),
                remote(crossed, recv_r.at[s, :, mine], cross_send.at[1, extra], cross_recv.at[1, extra], across[1]),
            ),
        )

    def launch(slot):
        pl.when(has_right)(lambda: [copy.start() for copy in slot[0]] and None)
        pl.when(has_left)(lambda: [copy.start() for copy in slot[1]] and None)

    def sent(slot):
        pl.when(has_right)(lambda: [copy.wait_send() for copy in slot[0]] and None)
        pl.when(has_left)(lambda: [copy.wait_send() for copy in slot[1]] and None)

    def arrived(slot):
        pl.when(has_left)(lambda: [copy.wait_recv() for copy in slot[0]] and None)
        pl.when(has_right)(lambda: [copy.wait_recv() for copy in slot[1]] and None)

    def early_slot(s):
        return halved_slot(s, s, own.at[s, :, mine], stage.at[s])

    def late_slot(s):
        h = s - LAG
        return halved_slot(s, s - HEADS + LAG, res_nb.at[h, :, mine], res_nb.at[h, :, theirs])

    def hand_back(h):
        return remote(fin_out.at[h], fin_in.at[h], fin_send.at[h], fin_recv.at[h], sibling)

    def hand_raw(h):
        return remote(res_own.at[h, :, theirs], fin_in.at[h], fin_send.at[h], fin_recv.at[h], sibling)

    def packed(pair, half):
        lanes = pl.ds(pl.multiple_of(pair * 2 * DH, 2 * DH), 2 * DH)
        q, k, v, g = [loaded[i, :, lanes] for i in range(4)]
        return join(q, g, half), join(k, v, half)

    def pack(pair, _):
        for half in range(2):
            h = 2 * pair + half
            a, b = packed((1 - core) * (HEADS // 2) + pair, half)
            stage[h, 0] = a
            stage[h, 1] = b
            a, b = packed(core * (HEADS // 2) + pair, half)
            own[h, 0, mine] = a
            own[h, 1, mine] = b
        return 0

    for load in loads:
        load.wait()
    pack(0, 0)
    pl.semaphore_wait(barrier, 1 + 2 * has_left.astype(jnp.int32) + 2 * has_right.astype(jnp.int32))
    launch(early_slot(0))
    launch(early_slot(1))
    exchange(0).start()
    exchange(1).start()
    pack(1, 0)
    launch(early_slot(2))
    exchange(2).start()
    exchange(3).start()

    def pack_rest(pair, _):
        pack(pair, 0)
        exchange(2 * pair).start()
        exchange(2 * pair + 1).start()
        return 0

    lax.fori_loop(2, HEADS // 2, pack_rest, 0)

    len_load.wait()
    here = chip.astype(F32)
    total = float(n * ROWS)
    docs = len_ref.shape[1]
    over = lax.broadcasted_iota(jnp.int32, (docs, docs), 1)
    down = lax.broadcasted_iota(jnp.int32, (docs, docs), 0)
    lengths = jnp.broadcast_to(len_ref[...].astype(F32), (docs, docs))
    ends_col = jnp.sum(jnp.where(over <= down, lengths, 0.0), axis=1, keepdims=True)
    ends_row = jnp.sum(jnp.where(over == down, ends_col, 0.0), axis=0, keepdims=True)
    for axis, ends in ((1, ends_col), (0, ends_row)):
        start_o, owner_o = token_info(ends, here * CHIP, axis, total)
        start_l, owner_l = token_info(ends, (here - 1.0) * CHIP, axis, total)
        start_r, owner_r = token_info(ends, (here + 1.0) * CHIP, axis, total)
        id_own = jnp.where(owner_o == here, start_o, -1.0)
        id_nb = jnp.where(owner_l == here, start_l, jnp.where(owner_r == here, start_r, -2.0))
        if axis == 1:
            id_row[:, 0:CHIP] = id_own
            id_row[:, CHIP:] = id_nb
        else:
            id_col[0:CHIP] = jnp.broadcast_to(id_own, (CHIP, 128))
            id_col[CHIP:] = jnp.broadcast_to(id_nb, (CHIP, 128))
            home[...] = jnp.broadcast_to(owner_o - here, (CHIP, 128)).astype(BF16)
            came = jnp.where(owner_l == here, -1.0, jnp.where(owner_r == here, 1.0, 0.0))
            guest[...] = jnp.broadcast_to(came, (CHIP, 128)).astype(BF16)

    def attend(t):
        came = guest[...]
        zero = jnp.zeros((CHIP, 2 * DH), BF16)
        both = []
        for i in range(2):
            nb = jnp.where(came < 0, recv_l[t, i], jnp.where(came > 0, recv_r[t, i], zero))
            both.append(jnp.concatenate([own[t, i], nb], axis=0))
        a, b = both
        at = a.T
        bt = b.T
        none = jnp.zeros((DH, 2 * CHIP), BF16)
        qt = jnp.concatenate([at[:DH], none], axis=0)
        gt = jnp.concatenate([none, at[DH:]], axis=0)
        ids = jnp.concatenate([id_col[...]] * (2 * CHIP // 128), axis=1)
        scores = jnp.dot(b, qt, preferred_element_type=F32)
        prob_grads = jnp.dot(b, gt, preferred_element_type=F32)
        scores = jnp.where(ids == id_row[...], scores, -jnp.inf)
        top = jnp.max(scores, axis=0, keepdims=True)
        grown = jnp.exp2((scores - top) * (LOG2E / 8.0))
        probs = grown * (1.0 / jnp.sum(grown, axis=0, keepdims=True))
        probs_low = probs.astype(BF16)
        out = jnp.dot(bt[DH:], probs_low, preferred_element_type=F32).astype(BF16).astype(F32)
        delta = jnp.sum(out * at[DH:].astype(F32), axis=0, keepdims=True)
        score_grads = (probs * (prob_grads - delta)).astype(BF16)
        dq = jnp.dot(bt[:DH], score_grads, preferred_element_type=F32) * 0.125
        first = jnp.concatenate([dq, out], axis=0).astype(BF16).T
        dk = jnp.dot(score_grads, a, preferred_element_type=F32) * 0.125
        dv = jnp.dot(probs_low, a, preferred_element_type=F32)
        second = jnp.where(low_lanes((2 * CHIP, 2 * DH)), dk, dv).astype(BF16)
        for i, result in enumerate((first, second)):
            res_own[t, i] = result[:CHIP]
            res_nb[t, i] = result[CHIP:]

    def settle(h, at, rows, mid, out):
        for i in range(2):
            out[h, i] = jnp.where(
                at > 0, recv_r[h + LAG, i, rows], jnp.where(at < 0, recv_l[h + LAG, i, rows], mid[i])
            )

    def step(t, _):
        @pl.when(t < LAG)
        def _():
            arrived(early_slot(t))
            exchange(t).wait_recv()

        @pl.when(t >= LAG)
        def _():
            arrived(whole_slot(t, own.at[0], own.at[0]))

        attend(t)
        s = t + LAG

        @pl.when(s < HEADS)
        def _():
            exchange(s).wait_recv()
            at = home[...]
            for i in range(2):
                send_r[t, i] = jnp.where(at > 0, own[s, i], res_nb[t, i])
                send_l[t, i] = jnp.where(at < 0, own[s, i], res_nb[t, i])
            launch(whole_slot(s, send_r.at[t], send_l.at[t]))

        @pl.when(s >= HEADS)
        def _():
            launch(late_slot(s))
            hand_raw(t).start()

        @pl.when(t >= LAG)
        def _():
            h = t - LAG
            settle(h, home[theirs], theirs, res_own.at[h, :, theirs], fin_out)
            hand_back(h).start()
            settle(h, home[mine], mine, res_own.at[h, :, mine], fin)

        return 0

    lax.fori_loop(0, HEADS, step, 0)

    def unpack(source, pair, place):
        lanes = pl.ds(pl.multiple_of(place * 2 * DH, 2 * DH), 2 * DH)
        e, o = 2 * pair, 2 * pair + 1
        dq_ref[:, lanes] = join(source[e, 0], source[o, 0], 0)
        o_ref[:, lanes] = join(source[e, 0], source[o, 0], 1)
        dk_ref[:, lanes] = join(source[e, 1], source[o, 1], 0)
        dv_ref[:, lanes] = join(source[e, 1], source[o, 1], 1)

    def unpack_both(pair, _):
        unpack(fin, pair, core * (HEADS // 2) + pair)
        unpack(fin_in, pair, (1 - core) * (HEADS // 2) + pair)
        return 0

    def handed(h, _):
        hand_back(h).wait_recv()
        return 0

    lax.fori_loop(0, HEADS, handed, 0)
    settled = (HEADS - LAG) // 2
    lax.fori_loop(0, settled, unpack_both, 0)
    at = home[mine]
    for s in range(HEADS, SLOTS):
        h = s - LAG
        arrived(late_slot(s))
        settle(h, at, mine, res_own.at[h, :, mine], fin)
        settle(h, at, theirs, fin_in.at[h], fin_in)
        if h % 2:
            unpack_both(h // 2, 0)

    def drain(h, _):
        exchange(h).wait_send()
        hand_back(h).wait_send()
        return 0

    def drain_slots(s, _):
        sent(whole_slot(s, own.at[0], own.at[0]))
        return 0

    lax.fori_loop(0, HEADS, drain, 0)
    lax.fori_loop(LAG, HEADS, drain_slots, 0)
    for s in range(LAG):
        sent(early_slot(s))
        sent(late_slot(HEADS + s))


def write_out(*refs):
    sources, outs, sems = refs[:4], refs[4:8], refs[8]
    copies = [pltpu.make_async_copy(src, dst, sems.at[i]) for i, (src, dst) in enumerate(zip(sources, outs))]
    for copy in copies:
        copy.start()
    for copy in copies:
        copy.wait()


def on_device(queries, keys, values, cotangent, doc_lengths):
    n = lax.axis_size("ctx")
    block = (2, CHIP, 2 * DH)
    half = (2, ROWS, 2 * DH)
    vmem = pl.BlockSpec(memory_space=pltpu.VMEM)
    anywhere = pl.BlockSpec(memory_space=pl.ANY)
    pairs = 2 * CHIP * 2 * CHIP * HEADS
    outs = [jax.ShapeDtypeStruct(queries.shape, BF16)] * 4
    dma = pltpu.SemaphoreType.DMA
    queries, keys, values, cotangent, lengths = [
        pltpu.with_memory_space_constraint(x, pltpu.HBM)
        for x in (queries, keys, values, cotangent, doc_lengths.reshape(1, -1))
    ]
    results = pl.pallas_call(
        functools.partial(kernel, n),
        out_shape=[pltpu.VMEM(queries.shape, BF16)] * 4,
        in_specs=[anywhere] * 5,
        out_specs=[vmem] * 4,
        scratch_shapes=[
            pltpu.VMEM((4, *queries.shape), BF16),
            pltpu.VMEM((1, doc_lengths.shape[0]), jnp.int32),
            pltpu.VMEM((HEADS, *block), BF16),
            pltpu.VMEM((HEADS, *half), BF16),
            pltpu.VMEM((HEADS, *block), BF16),
            pltpu.VMEM((HEADS, *block), BF16),
            pltpu.VMEM((HEADS - LAG, *block), BF16),
            pltpu.VMEM((HEADS - LAG, *block), BF16),
            pltpu.VMEM((SLOTS, *block), BF16),
            pltpu.VMEM((SLOTS, *block), BF16),
            pltpu.VMEM((HEADS, *half), BF16),
            pltpu.VMEM((HEADS, *half), BF16),
            pltpu.VMEM((HEADS, *half), BF16),
            pltpu.VMEM((1, 2 * CHIP), F32),
            pltpu.VMEM((2 * CHIP, 128), F32),
            pltpu.VMEM((CHIP, 128), BF16),
            pltpu.VMEM((CHIP, 128), BF16),
            dma((5,)),
            dma((HEADS,)),
            dma((HEADS,)),
            dma((SLOTS,)),
            dma((SLOTS,)),
            dma((SLOTS,)),
            dma((SLOTS,)),
            dma((2, 2 * LAG)),
            dma((2, 2 * LAG)),
            dma((HEADS,)),
            dma((HEADS,)),
        ],
        compiler_params=pltpu.CompilerParams(
            collective_id=0, has_side_effects=True, vmem_limit_bytes=VMEM_LIMIT
        ),
        cost_estimate=pl.CostEstimate(flops=12 * DH * pairs, bytes_accessed=1 << 21, transcendentals=pairs),
    )(lengths, queries, keys, values, cotangent)
    return tuple(
        pl.pallas_call(
            write_out,
            out_shape=outs,
            in_specs=[vmem] * 4,
            out_specs=[anywhere] * 4,
            scratch_shapes=[dma((4,))],
            compiler_params=pltpu.CompilerParams(vmem_limit_bytes=16 * 1024 * 1024),
        )(*results)
    )


def solution(mesh):
    rows = P(("dp", "ctx"), None)
    return jax.shard_map(
        on_device,
        mesh=mesh,
        in_specs=(rows, rows, rows, rows, P("dp")),
        out_specs=(rows, rows, rows, rows),
        check_vma=False,
    )
```

```python
import functools

import jax
import jax.numpy as jnp
from jax import lax
from jax.experimental import pallas as pl
from jax.experimental.pallas import tpu as pltpu
from jax.sharding import PartitionSpec as P

H = 16
DH = 64
ROWS = 128
CHIP = 2 * ROWS
HEADS = H // 2
LAG = 3
SLOTS = HEADS + LAG
VMEM_LIMIT = 40 * 1024 * 1024
LOG2E = 1.4426950408889634
F32 = jnp.float32
BF16 = jnp.bfloat16


def low_lanes(shape):
    return lax.broadcasted_iota(jnp.int32, shape, 1) < DH


def join(left, right, half):
    lanes = slice(0, DH) if half == 0 else slice(DH, 2 * DH)
    return jnp.concatenate([left[:, lanes], right[:, lanes]], axis=1)


def token_info(ends, base, axis, total):
    shape = (CHIP, 1) if axis == 0 else (1, CHIP)
    place = lax.broadcasted_iota(jnp.int32, shape, axis).astype(F32) + base
    before = ends <= place
    start = jnp.max(jnp.where(before, ends, 0.0), axis=1 - axis, keepdims=True)
    end = jnp.min(jnp.where(before, 4.0 * total, ends), axis=1 - axis, keepdims=True)
    first = jnp.floor(start * (1.0 / CHIP))
    last = jnp.floor((end - 1.0) * (1.0 / CHIP))
    owner = jnp.minimum(first + 1.0, last)
    inside = (place >= 0.0) & (place < total)
    return start, jnp.where(inside, owner, -9.0)


def kernel(
    n,
    len_hbm,
    q_hbm,
    k_hbm,
    v_hbm,
    g_hbm,
    o_ref,
    dq_ref,
    dk_ref,
    dv_ref,
    loaded,
    len_ref,
    own,
    stage,
    res_own,
    res_nb,
    send_r,
    send_l,
    recv_l,
    recv_r,
    fin,
    fin_out,
    fin_in,
    id_row,
    id_col,
    home,
    guest,
    load_sem,
    sib_send,
    sib_recv,
    r_send,
    r_recv,
    l_send,
    l_recv,
    cross_send,
    cross_recv,
    fin_send,
    fin_recv,
):
    me = lax.axis_index("ctx")
    core = lax.rem(me, 2)
    chip = lax.div(me, 2)
    sibling = me + 1 - 2 * core
    right = lax.rem(me + 2, n)
    left = lax.rem(me + n - 2, n)
    across = (lax.rem(sibling + 2, n), lax.rem(sibling + n - 2, n))
    mine = pl.ds(pl.multiple_of(core * ROWS, ROWS), ROWS)
    theirs = pl.ds(pl.multiple_of((1 - core) * ROWS, ROWS), ROWS)

    has_left = chip > 0
    has_right = chip < n // 2 - 1
    barrier = pltpu.get_barrier_semaphore()

    def greet(others):
        for other in others:
            pl.semaphore_signal(barrier, inc=1, device_id={"ctx": other}, device_id_type=pl.DeviceIdType.MESH)

    greet((sibling,))
    pl.when(has_right)(lambda: greet((right, across[0])))
    pl.when(has_left)(lambda: greet((left, across[1])))

    loads = [
        pltpu.make_async_copy(src, loaded.at[i], load_sem.at[i]) for i, src in enumerate((q_hbm, k_hbm, v_hbm, g_hbm))
    ]
    len_load = pltpu.make_async_copy(len_hbm, len_ref, load_sem.at[4])
    for load in (*loads, len_load):
        load.start()

    def remote(src, dst, send_sem, recv_sem, target):
        return pltpu.make_async_remote_copy(
            src_ref=src,
            dst_ref=dst,
            send_sem=send_sem,
            recv_sem=recv_sem,
            device_id={"ctx": target},
            device_id_type=pl.DeviceIdType.MESH,
        )

    def exchange(h):
        return remote(stage.at[h], own.at[h, :, mine], sib_send.at[h], sib_recv.at[h], sibling)

    def whole_slot(s, src_r, src_l):
        return (
            (remote(src_r, recv_l.at[s], r_send.at[s], r_recv.at[s], right),),
            (remote(src_l, recv_r.at[s], l_send.at[s], l_recv.at[s], left),),
        )

    def halved_slot(s, extra, straight, crossed):
        return (
            (
                remote(straight, recv_l.at[s, :, mine], r_send.at[s], r_recv.at[s], right),
                remote(crossed, recv_l.at[s, :, mine], cross_send.at[0, extra], cross_recv.at[0, extra], across[0]),
            ),
            (
                remote(straight, recv_r.at[s, :, mine], l_send.at[s], l_recv.at[s], left),
                remote(crossed, recv_r.at[s, :, mine], cross_send.at[1, extra], cross_recv.at[1, extra], across[1]),
            ),
        )

    def launch(slot):
        pl.when(has_right)(lambda: [copy.start() for copy in slot[0]] and None)
        pl.when(has_left)(lambda: [copy.start() for copy in slot[1]] and None)

    def sent(slot):
        pl.when(has_right)(lambda: [copy.wait_send() for copy in slot[0]] and None)
        pl.when(has_left)(lambda: [copy.wait_send() for copy in slot[1]] and None)

    def arrived(slot):
        pl.when(has_left)(lambda: [copy.wait_recv() for copy in slot[0]] and None)
        pl.when(has_right)(lambda: [copy.wait_recv() for copy in slot[1]] and None)

    def early_slot(s):
        return halved_slot(s, s, own.at[s, :, mine], stage.at[s])

    def late_slot(s):
        h = s - LAG
        return halved_slot(s, s - HEADS + LAG, res_nb.at[h, :, mine], res_nb.at[h, :, theirs])

    def hand_back(h):
        return remote(fin_out.at[h], fin_in.at[h], fin_send.at[h], fin_recv.at[h], sibling)

    def hand_raw(h):
        return remote(res_own.at[h, :, theirs], fin_in.at[h], fin_send.at[h], fin_recv.at[h], sibling)

    def packed(pair, half):
        lanes = pl.ds(pl.multiple_of(pair * 2 * DH, 2 * DH), 2 * DH)
        q, k, v, g = [loaded[i, :, lanes] for i in range(4)]
        return join(q, g, half), join(k, v, half)

    def pack(pair, _):
        for half in range(2):
            h = 2 * pair + half
            a, b = packed((1 - core) * (HEADS // 2) + pair, half)
            stage[h, 0] = a
            stage[h, 1] = b
            a, b = packed(core * (HEADS // 2) + pair, half)
            own[h, 0, mine] = a
            own[h, 1, mine] = b
        return 0

    for load in loads:
        load.wait()
    pack(0, 0)
    pl.semaphore_wait(barrier, 1 + 2 * has_left.astype(jnp.int32) + 2 * has_right.astype(jnp.int32))
    launch(early_slot(0))
    launch(early_slot(1))
    exchange(0).start()
    exchange(1).start()
    pack(1, 0)
    launch(early_slot(2))
    exchange(2).start()
    exchange(3).start()

    def pack_rest(pair, _):
        pack(pair, 0)
        exchange(2 * pair).start()
        exchange(2 * pair + 1).start()
        return 0

    lax.fori_loop(2, HEADS // 2, pack_rest, 0)

    len_load.wait()
    here = chip.astype(F32)
    total = float(n * ROWS)
    docs = len_ref.shape[1]
    over = lax.broadcasted_iota(jnp.int32, (docs, docs), 1)
    down = lax.broadcasted_iota(jnp.int32, (docs, docs), 0)
    lengths = jnp.broadcast_to(len_ref[...].astype(F32), (docs, docs))
    ends_col = jnp.sum(jnp.where(over <= down, lengths, 0.0), axis=1, keepdims=True)
    ends_row = jnp.sum(jnp.where(over == down, ends_col, 0.0), axis=0, keepdims=True)
    for axis, ends in ((1, ends_col), (0, ends_row)):
        start_o, owner_o = token_info(ends, here * CHIP, axis, total)
        start_l, owner_l = token_info(ends, (here - 1.0) * CHIP, axis, total)
        start_r, owner_r = token_info(ends, (here + 1.0) * CHIP, axis, total)
        id_own = jnp.where(owner_o == here, start_o, -1.0)
        id_nb = jnp.where(owner_l == here, start_l, jnp.where(owner_r == here, start_r, -2.0))
        if axis == 1:
            id_row[:, 0:CHIP] = id_own
            id_row[:, CHIP:] = id_nb
        else:
            id_col[0:CHIP] = jnp.broadcast_to(id_own, (CHIP, 128))
            id_col[CHIP:] = jnp.broadcast_to(id_nb, (CHIP, 128))
            home[...] = jnp.broadcast_to(owner_o - here, (CHIP, 128)).astype(BF16)
            came = jnp.where(owner_l == here, -1.0, jnp.where(owner_r == here, 1.0, 0.0))
            guest[...] = jnp.broadcast_to(came, (CHIP, 128)).astype(BF16)

    def turned(a, b):
        at, bt = a.T, b.T
        none = jnp.zeros((DH, CHIP), BF16)
        return at, bt, jnp.concatenate([at[:DH], none], axis=0), jnp.concatenate([none, at[DH:]], axis=0)

    def masked(b, qt, keys, queries):
        ids = jnp.concatenate([id_col[keys]] * 2, axis=1)
        return jnp.where(ids == id_row[:, queries], jnp.dot(b, qt, preferred_element_type=F32), -jnp.inf)

    ours, nbs = slice(0, CHIP), slice(CHIP, 2 * CHIP)
    rate = LOG2E / 8.0

    def prepare(t):
        a, b = own[t, 0], own[t, 1]
        at, bt, qt, gt = turned(a, b)
        scores = masked(b, qt, ours, ours)
        top = jnp.max(scores, axis=0, keepdims=True)
        grown = jnp.exp2((scores - top) * rate)
        total = jnp.sum(grown, axis=0, keepdims=True)
        return a, b, at, bt, qt, gt, top, grown, total, jnp.dot(b, gt, preferred_element_type=F32)

    def attend(t, prepared):
        a_o, b_o, at_o, bt_o, qt_o, gt_o, top_o, grown_o, total_o, prob_grads_o = prepared
        came = guest[...]
        zero = jnp.zeros((CHIP, 2 * DH), BF16)
        a_n, b_n = [
            jnp.where(came < 0, recv_l[t, i], jnp.where(came > 0, recv_r[t, i], zero)) for i in range(2)
        ]
        at_n, bt_n, qt_n, gt_n = turned(a_n, b_n)
        a = jnp.concatenate([a_o, a_n], axis=0)
        b = jnp.concatenate([b_o, b_n], axis=0)
        at = jnp.concatenate([at_o, at_n], axis=1)
        bt = jnp.concatenate([bt_o, bt_n], axis=1)
        scores = masked(b_n, qt_o, nbs, ours)
        scores_n = masked(b, qt_n, slice(0, 2 * CHIP), nbs)
        prob_grads = jnp.concatenate(
            [
                jnp.concatenate([prob_grads_o, jnp.dot(b_n, gt_o, preferred_element_type=F32)], axis=0),
                jnp.dot(b, gt_n, preferred_element_type=F32),
            ],
            axis=1,
        )
        top = jnp.maximum(top_o, jnp.max(scores, axis=0, keepdims=True))
        grown = jnp.exp2((scores - top) * rate)
        shrink = jnp.exp2((top_o - top) * rate)
        share = 1.0 / (total_o * shrink + jnp.sum(grown, axis=0, keepdims=True))
        probs_o = jnp.concatenate([grown_o * (shrink * share), grown * share], axis=0)
        top_n = jnp.max(scores_n, axis=0, keepdims=True)
        grown_n = jnp.exp2((scores_n - top_n) * rate)
        probs_n = grown_n * (1.0 / jnp.sum(grown_n, axis=0, keepdims=True))
        probs = jnp.concatenate([probs_o, probs_n], axis=1)
        probs_low = probs.astype(BF16)
        out = jnp.dot(bt[DH:], probs_low, preferred_element_type=F32).astype(BF16).astype(F32)
        delta = jnp.sum(out * at[DH:].astype(F32), axis=0, keepdims=True)
        score_grads = (probs * (prob_grads - delta)).astype(BF16)
        dq = jnp.dot(bt[:DH], score_grads, preferred_element_type=F32) * 0.125
        first = jnp.concatenate([dq, out], axis=0).astype(BF16).T
        dk = jnp.dot(score_grads, a, preferred_element_type=F32) * 0.125
        dv = jnp.dot(probs_low, a, preferred_element_type=F32)
        second = jnp.where(low_lanes((2 * CHIP, 2 * DH)), dk, dv).astype(BF16)
        for i, result in enumerate((first, second)):
            res_own[t, i] = result[:CHIP]
            res_nb[t, i] = result[CHIP:]

    def settle(h, at, rows, mid, out):
        for i in range(2):
            out[h, i] = jnp.where(
                at > 0, recv_r[h + LAG, i, rows], jnp.where(at < 0, recv_l[h + LAG, i, rows], mid[i])
            )

    def step(t, _):
        @pl.when(t < LAG)
        def _():
            exchange(t).wait_recv()

        prepared = prepare(t)

        @pl.when(t < LAG)
        def _():
            arrived(early_slot(t))

        @pl.when(t >= LAG)
        def _():
            arrived(whole_slot(t, own.at[0], own.at[0]))

        attend(t, prepared)
        s = t + LAG

        @pl.when(s < HEADS)
        def _():
            exchange(s).wait_recv()
            at = home[...]
            for i in range(2):
                send_r[t, i] = jnp.where(at > 0, own[s, i], res_nb[t, i])
                send_l[t, i] = jnp.where(at < 0, own[s, i], res_nb[t, i])
            launch(whole_slot(s, send_r.at[t], send_l.at[t]))

        @pl.when(s >= HEADS)
        def _():
            launch(late_slot(s))
            hand_raw(t).start()

        @pl.when(t >= LAG)
        def _():
            h = t - LAG
            settle(h, home[theirs], theirs, res_own.at[h, :, theirs], fin_out)
            hand_back(h).start()
            settle(h, home[mine], mine, res_own.at[h, :, mine], fin)

        return 0

    lax.fori_loop(0, HEADS, step, 0)

    def unpack(source, pair, place):
        lanes = pl.ds(pl.multiple_of(place * 2 * DH, 2 * DH), 2 * DH)
        e, o = 2 * pair, 2 * pair + 1
        dq_ref[:, lanes] = join(source[e, 0], source[o, 0], 0)
        o_ref[:, lanes] = join(source[e, 0], source[o, 0], 1)
        dk_ref[:, lanes] = join(source[e, 1], source[o, 1], 0)
        dv_ref[:, lanes] = join(source[e, 1], source[o, 1], 1)

    def unpack_both(pair, _):
        unpack(fin, pair, core * (HEADS // 2) + pair)
        unpack(fin_in, pair, (1 - core) * (HEADS // 2) + pair)
        return 0

    def handed(h, _):
        hand_back(h).wait_recv()
        return 0

    lax.fori_loop(0, HEADS, handed, 0)
    settled = (HEADS - LAG) // 2
    lax.fori_loop(0, settled, unpack_both, 0)
    at = home[mine]
    for s in range(HEADS, SLOTS):
        h = s - LAG
        arrived(late_slot(s))
        settle(h, at, mine, res_own.at[h, :, mine], fin)
        settle(h, at, theirs, fin_in.at[h], fin_in)
        if h % 2:
            unpack_both(h // 2, 0)

    def drain(h, _):
        exchange(h).wait_send()
        hand_back(h).wait_send()
        return 0

    def drain_slots(s, _):
        sent(whole_slot(s, own.at[0], own.at[0]))
        return 0

    lax.fori_loop(0, HEADS, drain, 0)
    lax.fori_loop(LAG, HEADS, drain_slots, 0)
    for s in range(LAG):
        sent(early_slot(s))
        sent(late_slot(HEADS + s))


def write_out(*refs):
    sources, outs, sems = refs[:4], refs[4:8], refs[8]
    copies = [pltpu.make_async_copy(src, dst, sems.at[i]) for i, (src, dst) in enumerate(zip(sources, outs))]
    for copy in copies:
        copy.start()
    for copy in copies:
        copy.wait()


def on_device(queries, keys, values, cotangent, doc_lengths):
    n = lax.axis_size("ctx")
    block = (2, CHIP, 2 * DH)
    half = (2, ROWS, 2 * DH)
    vmem = pl.BlockSpec(memory_space=pltpu.VMEM)
    anywhere = pl.BlockSpec(memory_space=pl.ANY)
    pairs = 2 * CHIP * 2 * CHIP * HEADS
    outs = [jax.ShapeDtypeStruct(queries.shape, BF16)] * 4
    dma = pltpu.SemaphoreType.DMA
    queries, keys, values, cotangent, lengths = [
        pltpu.with_memory_space_constraint(x, pltpu.HBM)
        for x in (queries, keys, values, cotangent, doc_lengths.reshape(1, -1))
    ]
    results = pl.pallas_call(
        functools.partial(kernel, n),
        out_shape=[pltpu.VMEM(queries.shape, BF16)] * 4,
        in_specs=[anywhere] * 5,
        out_specs=[vmem] * 4,
        scratch_shapes=[
            pltpu.VMEM((4, *queries.shape), BF16),
            pltpu.VMEM((1, doc_lengths.shape[0]), jnp.int32),
            pltpu.VMEM((HEADS, *block), BF16),
            pltpu.VMEM((HEADS, *half), BF16),
            pltpu.VMEM((HEADS, *block), BF16),
            pltpu.VMEM((HEADS, *block), BF16),
            pltpu.VMEM((HEADS - LAG, *block), BF16),
            pltpu.VMEM((HEADS - LAG, *block), BF16),
            pltpu.VMEM((SLOTS, *block), BF16),
            pltpu.VMEM((SLOTS, *block), BF16),
            pltpu.VMEM((HEADS, *half), BF16),
            pltpu.VMEM((HEADS, *half), BF16),
            pltpu.VMEM((HEADS, *half), BF16),
            pltpu.VMEM((1, 2 * CHIP), F32),
            pltpu.VMEM((2 * CHIP, 128), F32),
            pltpu.VMEM((CHIP, 128), BF16),
            pltpu.VMEM((CHIP, 128), BF16),
            dma((5,)),
            dma((HEADS,)),
            dma((HEADS,)),
            dma((SLOTS,)),
            dma((SLOTS,)),
            dma((SLOTS,)),
            dma((SLOTS,)),
            dma((2, 2 * LAG)),
            dma((2, 2 * LAG)),
            dma((HEADS,)),
            dma((HEADS,)),
        ],
        compiler_params=pltpu.CompilerParams(
            collective_id=0, has_side_effects=True, vmem_limit_bytes=VMEM_LIMIT
        ),
        cost_estimate=pl.CostEstimate(flops=12 * DH * pairs, bytes_accessed=1 << 21, transcendentals=pairs),
    )(lengths, queries, keys, values, cotangent)
    return tuple(
        pl.pallas_call(
            write_out,
            out_shape=outs,
            in_specs=[vmem] * 4,
            out_specs=[anywhere] * 4,
            scratch_shapes=[dma((4,))],
            compiler_params=pltpu.CompilerParams(vmem_limit_bytes=16 * 1024 * 1024),
        )(*results)
    )


def solution(mesh):
    rows = P(("dp", "ctx"), None)
    return jax.shard_map(
        on_device,
        mesh=mesh,
        in_specs=(rows, rows, rows, rows, P("dp")),
        out_specs=(rows, rows, rows, rows),
        check_vma=False,
    )
```

```python
import functools

import jax
import jax.numpy as jnp
from jax import lax
from jax.experimental import pallas as pl
from jax.experimental.pallas import tpu as pltpu
from jax.sharding import PartitionSpec as P

H = 16
DH = 64
ROWS = 128
CHIP = 2 * ROWS
HEADS = H // 2
LAG = 3
SLOTS = HEADS + LAG
VMEM_LIMIT = 40 * 1024 * 1024
LOG2E = 1.4426950408889634
F32 = jnp.float32
BF16 = jnp.bfloat16


def low_lanes(shape):
    return lax.broadcasted_iota(jnp.int32, shape, 1) < DH


def join(left, right, half):
    lanes = slice(0, DH) if half == 0 else slice(DH, 2 * DH)
    return jnp.concatenate([left[:, lanes], right[:, lanes]], axis=1)


def token_info(ends, base, axis, total):
    shape = (CHIP, 1) if axis == 0 else (1, CHIP)
    place = lax.broadcasted_iota(jnp.int32, shape, axis).astype(F32) + base
    before = ends <= place
    start = jnp.max(jnp.where(before, ends, 0.0), axis=1 - axis, keepdims=True)
    end = jnp.min(jnp.where(before, 4.0 * total, ends), axis=1 - axis, keepdims=True)
    first = jnp.floor(start * (1.0 / CHIP))
    last = jnp.floor((end - 1.0) * (1.0 / CHIP))
    owner = jnp.minimum(first + 1.0, last)
    inside = (place >= 0.0) & (place < total)
    return start, jnp.where(inside, owner, -9.0)


def kernel(
    n,
    len_hbm,
    q_hbm,
    k_hbm,
    v_hbm,
    g_hbm,
    o_ref,
    dq_ref,
    dk_ref,
    dv_ref,
    loaded,
    len_ref,
    own,
    stage,
    res_own,
    res_nb,
    send_r,
    send_l,
    recv_l,
    recv_r,
    fin,
    fin_out,
    fin_in,
    id_row,
    id_col,
    home,
    guest,
    load_sem,
    sib_send,
    sib_recv,
    r_send,
    r_recv,
    l_send,
    l_recv,
    cross_send,
    cross_recv,
    fin_send,
    fin_recv,
):
    me = lax.axis_index("ctx")
    core = lax.rem(me, 2)
    chip = lax.div(me, 2)
    sibling = me + 1 - 2 * core
    right = lax.rem(me + 2, n)
    left = lax.rem(me + n - 2, n)
    across = (lax.rem(sibling + 2, n), lax.rem(sibling + n - 2, n))
    mine = pl.ds(pl.multiple_of(core * ROWS, ROWS), ROWS)
    theirs = pl.ds(pl.multiple_of((1 - core) * ROWS, ROWS), ROWS)

    has_left = chip > 0
    has_right = chip < n // 2 - 1
    barrier = pltpu.get_barrier_semaphore()

    def greet(others):
        for other in others:
            pl.semaphore_signal(barrier, inc=1, device_id={"ctx": other}, device_id_type=pl.DeviceIdType.MESH)

    greet((sibling,))
    pl.when(has_right)(lambda: greet((right, across[0])))
    pl.when(has_left)(lambda: greet((left, across[1])))

    loads = [
        pltpu.make_async_copy(src, loaded.at[i], load_sem.at[i]) for i, src in enumerate((q_hbm, k_hbm, v_hbm, g_hbm))
    ]
    len_load = pltpu.make_async_copy(len_hbm, len_ref, load_sem.at[4])
    for load in (*loads, len_load):
        load.start()

    def remote(src, dst, send_sem, recv_sem, target):
        return pltpu.make_async_remote_copy(
            src_ref=src,
            dst_ref=dst,
            send_sem=send_sem,
            recv_sem=recv_sem,
            device_id={"ctx": target},
            device_id_type=pl.DeviceIdType.MESH,
        )

    def exchange(h):
        return remote(stage.at[h], own.at[h, :, mine], sib_send.at[h], sib_recv.at[h], sibling)

    def whole_slot(s, src_r, src_l):
        return (
            (remote(src_r, recv_l.at[s], r_send.at[s], r_recv.at[s], right),),
            (remote(src_l, recv_r.at[s], l_send.at[s], l_recv.at[s], left),),
        )

    def halved_slot(s, extra, straight, crossed):
        return (
            (
                remote(straight, recv_l.at[s, :, mine], r_send.at[s], r_recv.at[s], right),
                remote(crossed, recv_l.at[s, :, mine], cross_send.at[0, extra], cross_recv.at[0, extra], across[0]),
            ),
            (
                remote(straight, recv_r.at[s, :, mine], l_send.at[s], l_recv.at[s], left),
                remote(crossed, recv_r.at[s, :, mine], cross_send.at[1, extra], cross_recv.at[1, extra], across[1]),
            ),
        )

    def launch(slot):
        if slot[0]:
            pl.when(has_right)(lambda: [copy.start() for copy in slot[0]] and None)
        if slot[1]:
            pl.when(has_left)(lambda: [copy.start() for copy in slot[1]] and None)

    def sent(slot):
        pl.when(has_right)(lambda: [copy.wait_send() for copy in slot[0]] and None)
        pl.when(has_left)(lambda: [copy.wait_send() for copy in slot[1]] and None)

    def arrived(slot):
        pl.when(has_left)(lambda: [copy.wait_recv() for copy in slot[0]] and None)
        pl.when(has_right)(lambda: [copy.wait_recv() for copy in slot[1]] and None)

    def early_slot(s):
        return halved_slot(s, s, own.at[s, :, mine], stage.at[s])

    def late_slot(s):
        h = s - LAG
        return halved_slot(s, s - HEADS + LAG, res_nb.at[h, :, mine], res_nb.at[h, :, theirs])

    def hand_back(h):
        return remote(fin_out.at[h], fin_in.at[h], fin_send.at[h], fin_recv.at[h], sibling)

    def hand_raw(h):
        return remote(res_own.at[h, :, theirs], fin_in.at[h], fin_send.at[h], fin_recv.at[h], sibling)

    def packed(pair, half):
        lanes = pl.ds(pl.multiple_of(pair * 2 * DH, 2 * DH), 2 * DH)
        q, k, v, g = [loaded[i, :, lanes] for i in range(4)]
        return join(q, g, half), join(k, v, half)

    def pack(pair, _):
        for half in range(2):
            h = 2 * pair + half
            a, b = packed((1 - core) * (HEADS // 2) + pair, half)
            stage[h, 0] = a
            stage[h, 1] = b
            a, b = packed(core * (HEADS // 2) + pair, half)
            own[h, 0, mine] = a
            own[h, 1, mine] = b
        return 0

    for load in loads:
        load.wait()
    pack(0, 0)
    pl.semaphore_wait(barrier, 1 + 2 * has_left.astype(jnp.int32) + 2 * has_right.astype(jnp.int32))
    launch(early_slot(0))
    launch(early_slot(1))
    exchange(0).start()
    exchange(1).start()
    pack(1, 0)
    launch(early_slot(2))
    exchange(2).start()
    exchange(3).start()

    def pack_rest(pair, _):
        pack(pair, 0)
        exchange(2 * pair).start()
        exchange(2 * pair + 1).start()
        return 0

    lax.fori_loop(2, HEADS // 2, pack_rest, 0)

    len_load.wait()
    here = chip.astype(F32)
    total = float(n * ROWS)
    docs = len_ref.shape[1]
    over = lax.broadcasted_iota(jnp.int32, (docs, docs), 1)
    down = lax.broadcasted_iota(jnp.int32, (docs, docs), 0)
    lengths = jnp.broadcast_to(len_ref[...].astype(F32), (docs, docs))
    ends_col = jnp.sum(jnp.where(over <= down, lengths, 0.0), axis=1, keepdims=True)
    ends_row = jnp.sum(jnp.where(over == down, ends_col, 0.0), axis=0, keepdims=True)
    for axis, ends in ((1, ends_col), (0, ends_row)):
        start_o, owner_o = token_info(ends, here * CHIP, axis, total)
        start_l, owner_l = token_info(ends, (here - 1.0) * CHIP, axis, total)
        start_r, owner_r = token_info(ends, (here + 1.0) * CHIP, axis, total)
        id_own = jnp.where(owner_o == here, start_o, -1.0)
        id_nb = jnp.where(owner_l == here, start_l, jnp.where(owner_r == here, start_r, -2.0))
        if axis == 1:
            id_row[:, 0:CHIP] = id_own
            id_row[:, CHIP:] = id_nb
        else:
            id_col[0:CHIP] = jnp.broadcast_to(id_own, (CHIP, 128))
            id_col[CHIP:] = jnp.broadcast_to(id_nb, (CHIP, 128))
            home[...] = jnp.broadcast_to(owner_o - here, (CHIP, 128)).astype(BF16)
            came = jnp.where(owner_l == here, -1.0, jnp.where(owner_r == here, 1.0, 0.0))
            guest[...] = jnp.broadcast_to(came, (CHIP, 128)).astype(BF16)

    def attend(t):
        came = guest[...]
        zero = jnp.zeros((CHIP, 2 * DH), BF16)
        both = []
        for i in range(2):
            nb = jnp.where(came < 0, recv_l[t, i], jnp.where(came > 0, recv_r[t, i], zero))
            both.append(jnp.concatenate([own[t, i], nb], axis=0))
        a, b = both
        at = a.T
        bt = b.T
        none = jnp.zeros((DH, 2 * CHIP), BF16)
        qt = jnp.concatenate([at[:DH], none], axis=0)
        gt = jnp.concatenate([none, at[DH:]], axis=0)
        ids = jnp.concatenate([id_col[...]] * (2 * CHIP // 128), axis=1)
        scores = jnp.dot(b, qt, preferred_element_type=F32)
        prob_grads = jnp.dot(b, gt, preferred_element_type=F32)
        scores = jnp.where(ids == id_row[...], scores, -jnp.inf)
        top = jnp.max(scores, axis=0, keepdims=True)
        grown = jnp.exp2((scores - top) * (LOG2E / 8.0))
        probs = grown * (1.0 / jnp.sum(grown, axis=0, keepdims=True))
        probs_low = probs.astype(BF16)
        out = jnp.dot(bt[DH:], probs_low, preferred_element_type=F32).astype(BF16).astype(F32)
        delta = jnp.sum(out * at[DH:].astype(F32), axis=0, keepdims=True)
        score_grads = (probs * (prob_grads - delta)).astype(BF16)
        dq = jnp.dot(bt[:DH], score_grads, preferred_element_type=F32) * 0.125
        first = jnp.concatenate([dq, out], axis=0).astype(BF16).T
        dk = jnp.dot(score_grads, a, preferred_element_type=F32) * 0.125
        dv = jnp.dot(probs_low, a, preferred_element_type=F32)
        second = jnp.where(low_lanes((2 * CHIP, 2 * DH)), dk, dv).astype(BF16)
        for i, result in enumerate((first, second)):
            res_own[t, i] = result[:CHIP]
            res_nb[t, i] = result[CHIP:]

    def settle(h, at, rows, mid, out):
        for i in range(2):
            out[h, i] = jnp.where(
                at > 0, recv_r[h + LAG, i, rows], jnp.where(at < 0, recv_l[h + LAG, i, rows], mid[i])
            )

    def step(t, _):
        @pl.when(t < LAG)
        def _():
            arrived(early_slot(t))
            exchange(t).wait_recv()

        @pl.when(t >= LAG)
        def _():
            arrived(whole_slot(t, own.at[0], own.at[0]))

        attend(t)
        s = t + LAG

        @pl.when(s < HEADS)
        def _():
            exchange(s).wait_recv()
            at = home[...]
            to_right, to_left = whole_slot(s, send_r.at[t], send_l.at[t])
            for i in range(2):
                send_r[t, i] = jnp.where(at > 0, own[s, i], res_nb[t, i])
            launch((to_right, ()))
            for i in range(2):
                send_l[t, i] = jnp.where(at < 0, own[s, i], res_nb[t, i])
            launch(((), to_left))

        @pl.when(s >= HEADS)
        def _():
            launch(late_slot(s))
            hand_raw(t).start()

        @pl.when(t >= LAG)
        def _():
            h = t - LAG
            settle(h, home[theirs], theirs, res_own.at[h, :, theirs], fin_out)
            hand_back(h).start()
            settle(h, home[mine], mine, res_own.at[h, :, mine], fin)

        return 0

    lax.fori_loop(0, HEADS, step, 0)

    def unpack(source, pair, place):
        lanes = pl.ds(pl.multiple_of(place * 2 * DH, 2 * DH), 2 * DH)
        e, o = 2 * pair, 2 * pair + 1
        dq_ref[:, lanes] = join(source[e, 0], source[o, 0], 0)
        o_ref[:, lanes] = join(source[e, 0], source[o, 0], 1)
        dk_ref[:, lanes] = join(source[e, 1], source[o, 1], 0)
        dv_ref[:, lanes] = join(source[e, 1], source[o, 1], 1)

    def unpack_both(pair, _):
        unpack(fin, pair, core * (HEADS // 2) + pair)
        unpack(fin_in, pair, (1 - core) * (HEADS // 2) + pair)
        return 0

    def handed(h, _):
        hand_back(h).wait_recv()
        return 0

    lax.fori_loop(0, HEADS, handed, 0)
    settled = (HEADS - LAG) // 2
    lax.fori_loop(0, settled, unpack_both, 0)
    at = home[mine]
    for s in range(HEADS, SLOTS):
        h = s - LAG
        arrived(late_slot(s))
        settle(h, at, mine, res_own.at[h, :, mine], fin)
        settle(h, at, theirs, fin_in.at[h], fin_in)
        if h % 2:
            unpack_both(h // 2, 0)

    def drain(h, _):
        exchange(h).wait_send()
        hand_back(h).wait_send()
        return 0

    def drain_slots(s, _):
        sent(whole_slot(s, own.at[0], own.at[0]))
        return 0

    lax.fori_loop(0, HEADS, drain, 0)
    lax.fori_loop(LAG, HEADS, drain_slots, 0)
    for s in range(LAG):
        sent(early_slot(s))
        sent(late_slot(HEADS + s))


def write_out(*refs):
    sources, outs, sems = refs[:4], refs[4:8], refs[8]
    copies = [pltpu.make_async_copy(src, dst, sems.at[i]) for i, (src, dst) in enumerate(zip(sources, outs))]
    for copy in copies:
        copy.start()
    for copy in copies:
        copy.wait()


def on_device(queries, keys, values, cotangent, doc_lengths):
    n = lax.axis_size("ctx")
    block = (2, CHIP, 2 * DH)
    half = (2, ROWS, 2 * DH)
    vmem = pl.BlockSpec(memory_space=pltpu.VMEM)
    anywhere = pl.BlockSpec(memory_space=pl.ANY)
    pairs = 2 * CHIP * 2 * CHIP * HEADS
    outs = [jax.ShapeDtypeStruct(queries.shape, BF16)] * 4
    dma = pltpu.SemaphoreType.DMA
    queries, keys, values, cotangent, lengths = [
        pltpu.with_memory_space_constraint(x, pltpu.HBM)
        for x in (queries, keys, values, cotangent, doc_lengths.reshape(1, -1))
    ]
    results = pl.pallas_call(
        functools.partial(kernel, n),
        out_shape=[pltpu.VMEM(queries.shape, BF16)] * 4,
        in_specs=[anywhere] * 5,
        out_specs=[vmem] * 4,
        scratch_shapes=[
            pltpu.VMEM((4, *queries.shape), BF16),
            pltpu.VMEM((1, doc_lengths.shape[0]), jnp.int32),
            pltpu.VMEM((HEADS, *block), BF16),
            pltpu.VMEM((HEADS, *half), BF16),
            pltpu.VMEM((HEADS, *block), BF16),
            pltpu.VMEM((HEADS, *block), BF16),
            pltpu.VMEM((HEADS - LAG, *block), BF16),
            pltpu.VMEM((HEADS - LAG, *block), BF16),
            pltpu.VMEM((SLOTS, *block), BF16),
            pltpu.VMEM((SLOTS, *block), BF16),
            pltpu.VMEM((HEADS, *half), BF16),
            pltpu.VMEM((HEADS, *half), BF16),
            pltpu.VMEM((HEADS, *half), BF16),
            pltpu.VMEM((1, 2 * CHIP), F32),
            pltpu.VMEM((2 * CHIP, 128), F32),
            pltpu.VMEM((CHIP, 128), BF16),
            pltpu.VMEM((CHIP, 128), BF16),
            dma((5,)),
            dma((HEADS,)),
            dma((HEADS,)),
            dma((SLOTS,)),
            dma((SLOTS,)),
            dma((SLOTS,)),
            dma((SLOTS,)),
            dma((2, 2 * LAG)),
            dma((2, 2 * LAG)),
            dma((HEADS,)),
            dma((HEADS,)),
        ],
        compiler_params=pltpu.CompilerParams(
            collective_id=0, has_side_effects=True, vmem_limit_bytes=VMEM_LIMIT
        ),
        cost_estimate=pl.CostEstimate(flops=12 * DH * pairs, bytes_accessed=1 << 21, transcendentals=pairs),
    )(lengths, queries, keys, values, cotangent)
    return tuple(
        pl.pallas_call(
            write_out,
            out_shape=outs,
            in_specs=[vmem] * 4,
            out_specs=[anywhere] * 4,
            scratch_shapes=[dma((4,))],
            compiler_params=pltpu.CompilerParams(vmem_limit_bytes=16 * 1024 * 1024),
        )(*results)
    )


def solution(mesh):
    rows = P(("dp", "ctx"), None)
    return jax.shard_map(
        on_device,
        mesh=mesh,
        in_specs=(rows, rows, rows, rows, P("dp")),
        out_specs=(rows, rows, rows, rows),
        check_vma=False,
    )
```

```python
import functools

import jax
import jax.numpy as jnp
from jax import lax
from jax.experimental import pallas as pl
from jax.experimental.pallas import tpu as pltpu
from jax.sharding import PartitionSpec as P

H = 16
DH = 64
ROWS = 128
CHIP = 2 * ROWS
HEADS = H // 2
LAG = 3
SLOTS = HEADS + LAG
VMEM_LIMIT = 40 * 1024 * 1024
LOG2E = 1.4426950408889634
F32 = jnp.float32
BF16 = jnp.bfloat16


def low_lanes(shape):
    return lax.broadcasted_iota(jnp.int32, shape, 1) < DH


def join(left, right, half):
    lanes = slice(0, DH) if half == 0 else slice(DH, 2 * DH)
    return jnp.concatenate([left[:, lanes], right[:, lanes]], axis=1)


def token_info(ends, base, axis, total):
    shape = (CHIP, 1) if axis == 0 else (1, CHIP)
    place = lax.broadcasted_iota(jnp.int32, shape, axis).astype(F32) + base
    before = ends <= place
    start = jnp.max(jnp.where(before, ends, 0.0), axis=1 - axis, keepdims=True)
    end = jnp.min(jnp.where(before, 4.0 * total, ends), axis=1 - axis, keepdims=True)
    first = jnp.floor(start * (1.0 / CHIP))
    last = jnp.floor((end - 1.0) * (1.0 / CHIP))
    owner = jnp.minimum(first + 1.0, last)
    inside = (place >= 0.0) & (place < total)
    return start, jnp.where(inside, owner, -9.0)


def kernel(
    n,
    len_hbm,
    q_hbm,
    k_hbm,
    v_hbm,
    g_hbm,
    o_ref,
    dq_ref,
    dk_ref,
    dv_ref,
    loaded,
    len_ref,
    own,
    stage,
    res_own,
    res_nb,
    send_r,
    send_l,
    recv_l,
    recv_r,
    fin,
    fin_out,
    fin_in,
    id_row,
    id_col,
    home,
    guest,
    load_sem,
    sib_send,
    sib_recv,
    r_send,
    r_recv,
    l_send,
    l_recv,
    cross_send,
    cross_recv,
    fin_send,
    fin_recv,
):
    me = lax.axis_index("ctx")
    core = lax.rem(me, 2)
    chip = lax.div(me, 2)
    sibling = me + 1 - 2 * core
    right = lax.rem(me + 2, n)
    left = lax.rem(me + n - 2, n)
    across = (lax.rem(sibling + 2, n), lax.rem(sibling + n - 2, n))
    mine = pl.ds(pl.multiple_of(core * ROWS, ROWS), ROWS)
    theirs = pl.ds(pl.multiple_of((1 - core) * ROWS, ROWS), ROWS)

    has_left = chip > 0
    has_right = chip < n // 2 - 1
    barrier = pltpu.get_barrier_semaphore()

    def greet(others):
        for other in others:
            pl.semaphore_signal(barrier, inc=1, device_id={"ctx": other}, device_id_type=pl.DeviceIdType.MESH)

    greet((sibling,))
    pl.when(has_right)(lambda: greet((right, across[0])))
    pl.when(has_left)(lambda: greet((left, across[1])))

    loads = [
        pltpu.make_async_copy(src, loaded.at[i], load_sem.at[i]) for i, src in enumerate((q_hbm, k_hbm, v_hbm, g_hbm))
    ]
    len_load = pltpu.make_async_copy(len_hbm, len_ref, load_sem.at[4])
    for load in (*loads, len_load):
        load.start()

    def remote(src, dst, send_sem, recv_sem, target):
        return pltpu.make_async_remote_copy(
            src_ref=src,
            dst_ref=dst,
            send_sem=send_sem,
            recv_sem=recv_sem,
            device_id={"ctx": target},
            device_id_type=pl.DeviceIdType.MESH,
        )

    def exchange(h):
        return remote(stage.at[h], own.at[h, :, mine], sib_send.at[h], sib_recv.at[h], sibling)

    def whole_slot(s, src_r, src_l):
        return (
            (remote(src_r, recv_l.at[s], r_send.at[s], r_recv.at[s], right),),
            (remote(src_l, recv_r.at[s], l_send.at[s], l_recv.at[s], left),),
        )

    def halved_slot(s, extra, straight, crossed):
        return (
            (
                remote(straight, recv_l.at[s, :, mine], r_send.at[s], r_recv.at[s], right),
                remote(crossed, recv_l.at[s, :, mine], cross_send.at[0, extra], cross_recv.at[0, extra], across[0]),
            ),
            (
                remote(straight, recv_r.at[s, :, mine], l_send.at[s], l_recv.at[s], left),
                remote(crossed, recv_r.at[s, :, mine], cross_send.at[1, extra], cross_recv.at[1, extra], across[1]),
            ),
        )

    def launch(slot):
        if slot[0]:
            pl.when(has_right)(lambda: [copy.start() for copy in slot[0]] and None)
        if slot[1]:
            pl.when(has_left)(lambda: [copy.start() for copy in slot[1]] and None)

    def sent(slot):
        pl.when(has_right)(lambda: [copy.wait_send() for copy in slot[0]] and None)
        pl.when(has_left)(lambda: [copy.wait_send() for copy in slot[1]] and None)

    def arrived(slot):
        pl.when(has_left)(lambda: [copy.wait_recv() for copy in slot[0]] and None)
        pl.when(has_right)(lambda: [copy.wait_recv() for copy in slot[1]] and None)

    def early_slot(s):
        return halved_slot(s, s, own.at[s, :, mine], stage.at[s])

    def late_slot(s):
        h = s - LAG
        return halved_slot(s, s - HEADS + LAG, res_nb.at[h, :, mine], res_nb.at[h, :, theirs])

    def hand_back(h):
        return remote(fin_out.at[h], fin_in.at[h], fin_send.at[h], fin_recv.at[h], sibling)

    def hand_raw(h):
        return remote(res_own.at[h, :, theirs], fin_in.at[h], fin_send.at[h], fin_recv.at[h], sibling)

    def packed(pair, half):
        lanes = pl.ds(pl.multiple_of(pair * 2 * DH, 2 * DH), 2 * DH)
        q, k, v, g = [loaded[i, :, lanes] for i in range(4)]
        return join(q, g, half), join(k, v, half)

    def pack(pair, _):
        for half in range(2):
            h = 2 * pair + half
            a, b = packed((1 - core) * (HEADS // 2) + pair, half)
            stage[h, 0] = a
            stage[h, 1] = b
            a, b = packed(core * (HEADS // 2) + pair, half)
            own[h, 0, mine] = a
            own[h, 1, mine] = b
        return 0

    for load in loads:
        load.wait()
    pack(0, 0)
    pl.semaphore_wait(barrier, 1 + 2 * has_left.astype(jnp.int32) + 2 * has_right.astype(jnp.int32))
    launch(early_slot(0))
    launch(early_slot(1))
    exchange(0).start()
    exchange(1).start()
    pack(1, 0)
    launch(early_slot(2))
    exchange(2).start()
    exchange(3).start()

    def pack_rest(pair, _):
        pack(pair, 0)
        exchange(2 * pair).start()
        exchange(2 * pair + 1).start()
        return 0

    lax.fori_loop(2, HEADS // 2, pack_rest, 0)

    len_load.wait()
    here = chip.astype(F32)
    total = float(n * ROWS)
    docs = len_ref.shape[1]
    over = lax.broadcasted_iota(jnp.int32, (docs, docs), 1)
    down = lax.broadcasted_iota(jnp.int32, (docs, docs), 0)
    lengths = jnp.broadcast_to(len_ref[...].astype(F32), (docs, docs))
    ends_col = jnp.sum(jnp.where(over <= down, lengths, 0.0), axis=1, keepdims=True)
    ends_row = jnp.sum(jnp.where(over == down, ends_col, 0.0), axis=0, keepdims=True)
    for axis, ends in ((1, ends_col), (0, ends_row)):
        start_o, owner_o = token_info(ends, here * CHIP, axis, total)
        start_l, owner_l = token_info(ends, (here - 1.0) * CHIP, axis, total)
        start_r, owner_r = token_info(ends, (here + 1.0) * CHIP, axis, total)
        id_own = jnp.where(owner_o == here, start_o, -1.0)
        id_nb = jnp.where(owner_l == here, start_l, jnp.where(owner_r == here, start_r, -2.0))
        if axis == 1:
            id_row[:, 0:CHIP] = id_own
            id_row[:, CHIP:] = id_nb
        else:
            id_col[0:CHIP] = jnp.broadcast_to(id_own, (CHIP, 128))
            id_col[CHIP:] = jnp.broadcast_to(id_nb, (CHIP, 128))
            home[...] = jnp.broadcast_to(owner_o - here, (CHIP, 128)).astype(BF16)
            came = jnp.where(owner_l == here, -1.0, jnp.where(owner_r == here, 1.0, 0.0))
            guest[...] = jnp.broadcast_to(came, (CHIP, 128)).astype(BF16)

    def attend(t):
        came = guest[...]
        zero = jnp.zeros((CHIP, 2 * DH), BF16)
        both = []
        for i in range(2):
            nb = jnp.where(came < 0, recv_l[t, i], jnp.where(came > 0, recv_r[t, i], zero))
            both.append(jnp.concatenate([own[t, i], nb], axis=0))
        a, b = both
        at = a.T
        bt = b.T
        none = jnp.zeros((DH, 2 * CHIP), BF16)
        qt = jnp.concatenate([at[:DH], none], axis=0)
        gt = jnp.concatenate([none, at[DH:]], axis=0)
        ids = jnp.concatenate([id_col[...]] * (2 * CHIP // 128), axis=1)
        scores = jnp.dot(b, qt, preferred_element_type=F32)
        prob_grads = jnp.dot(b, gt, preferred_element_type=F32)
        scores = jnp.where(ids == id_row[...], scores, -jnp.inf)
        top = jnp.max(scores, axis=0, keepdims=True)
        grown = jnp.exp2((scores - top) * (LOG2E / 8.0))
        probs = grown * (1.0 / jnp.sum(grown, axis=0, keepdims=True))
        probs_low = probs.astype(BF16)
        out = jnp.dot(bt[DH:], probs_low, preferred_element_type=F32).astype(BF16).astype(F32)
        delta = jnp.sum(out * at[DH:].astype(F32), axis=0, keepdims=True)
        score_grads = (probs * (prob_grads - delta)).astype(BF16)
        dq = jnp.dot(bt[:DH], score_grads, preferred_element_type=F32) * 0.125
        first = jnp.concatenate([dq, out], axis=0).astype(BF16).T
        dk = jnp.dot(score_grads, a, preferred_element_type=F32) * 0.125
        dv = jnp.dot(probs_low, a, preferred_element_type=F32)
        second = jnp.where(low_lanes((2 * CHIP, 2 * DH)), dk, dv).astype(BF16)
        for i, result in enumerate((first, second)):
            res_own[t, i] = result[:CHIP]
            res_nb[t, i] = result[CHIP:]

    def settle(h, at, rows, mid, out):
        for i in range(2):
            out[h, i] = jnp.where(
                at > 0, recv_r[h + LAG, i, rows], jnp.where(at < 0, recv_l[h + LAG, i, rows], mid[i])
            )

    def step(t, _):
        @pl.when(t < LAG)
        def _():
            arrived(early_slot(t))
            exchange(t).wait_recv()

        @pl.when(t >= LAG)
        def _():
            arrived(whole_slot(t, own.at[0], own.at[0]))

        attend(t)
        s = t + LAG

        @pl.when(s < HEADS)
        def _():
            exchange(s).wait_recv()
            at = home[...]
            to_right, to_left = whole_slot(s, send_r.at[t], send_l.at[t])
            for i in range(2):
                send_r[t, i] = jnp.where(at > 0, own[s, i], res_nb[t, i])
            launch((to_right, ()))
            for i in range(2):
                send_l[t, i] = jnp.where(at < 0, own[s, i], res_nb[t, i])
            launch(((), to_left))

        @pl.when(s >= HEADS)
        def _():
            launch(late_slot(s))
            hand_raw(t).start()

        @pl.when(t >= LAG)
        def _():
            h = t - LAG
            settle(h, home[theirs], theirs, res_own.at[h, :, theirs], fin_out)
            hand_back(h).start()

        return 0

    lax.fori_loop(0, HEADS, step, 0)

    def unpack(source, pair, place):
        lanes = pl.ds(pl.multiple_of(place * 2 * DH, 2 * DH), 2 * DH)
        e, o = 2 * pair, 2 * pair + 1
        dq_ref[:, lanes] = join(source[e, 0], source[o, 0], 0)
        o_ref[:, lanes] = join(source[e, 0], source[o, 0], 1)
        dk_ref[:, lanes] = join(source[e, 1], source[o, 1], 0)
        dv_ref[:, lanes] = join(source[e, 1], source[o, 1], 1)

    def unpack_both(pair, _):
        unpack(fin, pair, core * (HEADS // 2) + pair)
        unpack(fin_in, pair, (1 - core) * (HEADS // 2) + pair)
        return 0

    def handed(h, _):
        hand_back(h).wait_recv()
        return 0

    def settle_mine(h, _):
        settle(h, home[mine], mine, res_own.at[h, :, mine], fin)
        return 0

    lax.fori_loop(0, HEADS - LAG, settle_mine, 0)
    lax.fori_loop(0, HEADS, handed, 0)
    settled = (HEADS - LAG) // 2
    lax.fori_loop(0, settled, unpack_both, 0)
    at = home[mine]
    for s in range(HEADS, SLOTS):
        h = s - LAG
        arrived(late_slot(s))
        settle(h, at, mine, res_own.at[h, :, mine], fin)
        settle(h, at, theirs, fin_in.at[h], fin_in)
        if h % 2:
            unpack_both(h // 2, 0)

    def drain(h, _):
        exchange(h).wait_send()
        hand_back(h).wait_send()
        return 0

    def drain_slots(s, _):
        sent(whole_slot(s, own.at[0], own.at[0]))
        return 0

    lax.fori_loop(0, HEADS, drain, 0)
    lax.fori_loop(LAG, HEADS, drain_slots, 0)
    for s in range(LAG):
        sent(early_slot(s))
        sent(late_slot(HEADS + s))


def write_out(*refs):
    sources, outs, sems = refs[:4], refs[4:8], refs[8]
    copies = [pltpu.make_async_copy(src, dst, sems.at[i]) for i, (src, dst) in enumerate(zip(sources, outs))]
    for copy in copies:
        copy.start()
    for copy in copies:
        copy.wait()


def on_device(queries, keys, values, cotangent, doc_lengths):
    n = lax.axis_size("ctx")
    block = (2, CHIP, 2 * DH)
    half = (2, ROWS, 2 * DH)
    vmem = pl.BlockSpec(memory_space=pltpu.VMEM)
    anywhere = pl.BlockSpec(memory_space=pl.ANY)
    pairs = 2 * CHIP * 2 * CHIP * HEADS
    outs = [jax.ShapeDtypeStruct(queries.shape, BF16)] * 4
    dma = pltpu.SemaphoreType.DMA
    queries, keys, values, cotangent, lengths = [
        pltpu.with_memory_space_constraint(x, pltpu.HBM)
        for x in (queries, keys, values, cotangent, doc_lengths.reshape(1, -1))
    ]
    results = pl.pallas_call(
        functools.partial(kernel, n),
        out_shape=[pltpu.VMEM(queries.shape, BF16)] * 4,
        in_specs=[anywhere] * 5,
        out_specs=[vmem] * 4,
        scratch_shapes=[
            pltpu.VMEM((4, *queries.shape), BF16),
            pltpu.VMEM((1, doc_lengths.shape[0]), jnp.int32),
            pltpu.VMEM((HEADS, *block), BF16),
            pltpu.VMEM((HEADS, *half), BF16),
            pltpu.VMEM((HEADS, *block), BF16),
            pltpu.VMEM((HEADS, *block), BF16),
            pltpu.VMEM((HEADS - LAG, *block), BF16),
            pltpu.VMEM((HEADS - LAG, *block), BF16),
            pltpu.VMEM((SLOTS, *block), BF16),
            pltpu.VMEM((SLOTS, *block), BF16),
            pltpu.VMEM((HEADS, *half), BF16),
            pltpu.VMEM((HEADS, *half), BF16),
            pltpu.VMEM((HEADS, *half), BF16),
            pltpu.VMEM((1, 2 * CHIP), F32),
            pltpu.VMEM((2 * CHIP, 128), F32),
            pltpu.VMEM((CHIP, 128), BF16),
            pltpu.VMEM((CHIP, 128), BF16),
            dma((5,)),
            dma((HEADS,)),
            dma((HEADS,)),
            dma((SLOTS,)),
            dma((SLOTS,)),
            dma((SLOTS,)),
            dma((SLOTS,)),
            dma((2, 2 * LAG)),
            dma((2, 2 * LAG)),
            dma((HEADS,)),
            dma((HEADS,)),
        ],
        compiler_params=pltpu.CompilerParams(
            collective_id=0, has_side_effects=True, vmem_limit_bytes=VMEM_LIMIT
        ),
        cost_estimate=pl.CostEstimate(flops=12 * DH * pairs, bytes_accessed=1 << 21, transcendentals=pairs),
    )(lengths, queries, keys, values, cotangent)
    return tuple(
        pl.pallas_call(
            write_out,
            out_shape=outs,
            in_specs=[vmem] * 4,
            out_specs=[anywhere] * 4,
            scratch_shapes=[dma((4,))],
            compiler_params=pltpu.CompilerParams(vmem_limit_bytes=16 * 1024 * 1024),
        )(*results)
    )


def solution(mesh):
    rows = P(("dp", "ctx"), None)
    return jax.shard_map(
        on_device,
        mesh=mesh,
        in_specs=(rows, rows, rows, rows, P("dp")),
        out_specs=(rows, rows, rows, rows),
        check_vma=False,
    )
```
